512 devices in a mesh: ctx: 64 (over x, z), head: 2 (over core), seq: 4 (over y).
Axes of the slice: x: 4, y: 4, z: 16, core: 2. Of those that a mesh axis runs over, the one named last changes fastest.
Arguments:
- mixer_input: bfloat16 [32768, 5120], P(('seq', 'ctx'), 'head'), parts along dimension 0, may hold values from -6 to 6
- gate_input: bfloat16 [32768, 5120], P(('seq', 'ctx'), 'head'), parts along dimension 0, may hold values from -12 to 12
- input_proj: bfloat16 [32768, 128], P(('seq', 'ctx')), parts along dimension 0, may hold values from -0.5 to 0.5
- output_proj: bfloat16 [32768, 128], P(('seq', 'ctx')), parts along dimension 0, may hold values from -20 to 20
- step_size: float32 [80, 32768], P('head', ('seq', 'ctx')), parts along dimension 1, may hold values from 0 to 1, as said below
- decay_log: float32 [80, 32768], P('head', ('seq', 'ctx')), parts along dimension 1, may hold values from -2 to 0, as said below
- level_weight: float32 [7, 80, 32768], P(None, 'head', ('seq', 'ctx')), parts along dimension 2, may hold values from 0.25 to 2.5
- norm_weight: float32 [5120], P('head'), may hold values from 0.1 to 1.9
Outputs:
- mixed_out: bfloat16 [32768, 5120], P(('seq', 'ctx'), 'head'), parts along dimension 0
The draws below stay inside these ranges and needn't reach their ends.
There are 4 independent parts, one for each index of `seq`. The reference program is written for one: setup_inputs(seed, part) draws one part's arguments, and reference() takes and returns one part's arrays. A program takes and returns all parts, laid end to end along the dimension named above; an argument that names none is the same for every part. Nothing has to cross between parts.
Inputs may be any that keep to these rules, and one draw needn't show every extreme that they name: `step_size`: positive. `decay_log`: never positive.
All inputs are finite; a program needn't handle non-finite values.
Results may differ from the reference program's by a relative error of at most 0.0058.
Values may be sent and summed in bfloat16 or wider, within the bound.
No kernel may reach another device: no remote copies, remote signals or barrier semaphores. Data moves between devices by JAX's collectives and lax.ppermute only.
A program may use at most 64 MiB of HBM per device.

```python
import math
import jax
import jax.numpy as jnp
from jax import lax

HEADS = 80
HEADDIM = 64
STATE = 128
BLOCK = 128
TOK_DEV = 128
INNER = 5120
SEQUENCE_TOKENS = 8192
LEVELS = 7


def head_rates(key, fast_share):
    key_slow, key_fast, key_pick = jax.random.split(key, 3)
    slow_rate = jax.random.uniform(key_slow, (HEADS,), jnp.float32, 0.1, 0.5) / SEQUENCE_TOKENS
    fast_rate = jnp.exp(jax.random.uniform(key_fast, (HEADS,), jnp.float32, math.log(1.0 / 50.0), math.log(1.0 / 30.0)))
    picked = jax.random.randint(key_pick, (HEADS,), 0, 10)
    return jnp.where(picked < fast_share, fast_rate, slow_rate)


def draw_decay_log(key, part):
    steady_level = head_rates(key, 5)
    key = jax.random.fold_in(key, 11)
    key_tok, key_dev, key_pos, key_size = jax.random.split(key, 4)
    small_perturbation = jnp.exp(jax.random.uniform(key_tok, (HEADS, SEQUENCE_TOKENS), jnp.float32, -0.7, 0.7))
    token_groupings = jnp.exp(jax.random.uniform(key_dev, (HEADS, SEQUENCE_TOKENS // TOK_DEV), jnp.float32, -0.7, 0.7))
    token_groupings = jnp.repeat(token_groupings, TOK_DEV, axis=1)
    target_locations = jax.random.randint(key_pos, (3,), 0, SEQUENCE_TOKENS)
    spike_amounts = jax.random.uniform(key_size, (HEADS, 3), jnp.float32, 0.22, 0.5)
    spike_positions = (jnp.arange(SEQUENCE_TOKENS)[None, :] == target_locations[:, None]).astype(jnp.float32)
    spike_events = jnp.sum(spike_amounts[:, :, None] * spike_positions[None, :, :], axis=1)
    return (-(steady_level[:, None] * small_perturbation * token_groupings + spike_events)).astype(jnp.float32)


def draw_step_size(key, part):
    steady_level = head_rates(key, 5)
    key = jax.random.fold_in(key, 12)
    small_perturbation = jnp.exp(jax.random.uniform(key, (HEADS, SEQUENCE_TOKENS), jnp.float32, -0.7, 0.7))
    return (jnp.sqrt(2.0 * steady_level)[:, None] * small_perturbation).astype(jnp.float32)


def draw_gate_input(key, part):
    key = jax.random.fold_in(key, 13)
    key_val, key_col = jax.random.split(key)
    head_place = (jnp.arange(INNER) // HEADDIM).astype(jnp.float32) / (HEADS - 1)
    column = 0.5 * 3.0 ** head_place
    noise_draw = jnp.clip(jax.random.normal(key_val, (SEQUENCE_TOKENS, INNER), jnp.float32), -5.0, 5.0)
    column = column * jnp.exp(jax.random.uniform(key_col, (INNER,), jnp.float32, -0.4, 0.4))
    return (noise_draw * column[None, :]).astype(jnp.bfloat16)


def draw_output_proj(key, part):
    key = jax.random.fold_in(key, 14)
    key_val, key_row = jax.random.split(key)
    row_scale = jnp.exp(jax.random.uniform(key_row, (SEQUENCE_TOKENS,), jnp.float32, math.log(0.4), math.log(4.0)))
    noise_draw = jnp.clip(jax.random.normal(key_val, (SEQUENCE_TOKENS, STATE), jnp.float32), -5.0, 5.0)
    return (noise_draw * row_scale[:, None]).astype(jnp.bfloat16)


def level_of(own_key, dims, cuts, low, top_value):
    loudness = 1.0
    for position, parts in cuts:
        draws = jax.random.uniform(jax.random.fold_in(jax.random.fold_in(own_key, 6), position), (parts,), jnp.float32, low / len(cuts), top_value / len(cuts))
        loudness = loudness * jnp.repeat(jnp.exp(draws), dims[position] // parts).reshape((-1,) + (1,) * (len(dims) - 1 - position))
    return loudness


def centred(key, dims, scale, most, cuts=(), kind=jnp.bfloat16):
    result = scale * jax.random.normal(key, dims, jnp.float32)
    if cuts:
        result = result * level_of(key, dims, cuts, -0.22, 0.18)
    return jnp.clip(result, -most, most).astype(kind)


def setup_inputs(seed: int = 0, part: int = 0) -> dict:
    key_list = jax.random.split(jax.random.key(seed), 9)
    own_keys = jax.random.split(jax.random.fold_in(key_list[8], part), 9)
    mixer_input = centred(own_keys[0], (SEQUENCE_TOKENS, INNER), 1.0, 6.0, ((0, 64), (1, 2)))
    gate_input = draw_gate_input(jax.random.fold_in(jax.random.fold_in(key_list[8], part), 71), part)
    input_proj = centred(own_keys[2], (SEQUENCE_TOKENS, STATE), STATE ** -0.5, 0.5, ((0, 64),))
    output_proj = draw_output_proj(jax.random.fold_in(jax.random.fold_in(key_list[8], part), 71), part)
    step_size = draw_step_size(jax.random.fold_in(jax.random.fold_in(key_list[8], part), 71), part)
    decay_log = draw_decay_log(jax.random.fold_in(jax.random.fold_in(key_list[8], part), 71), part)
    level_weight = jnp.clip(jnp.exp(math.log(2.5) - 2.3025851 * jax.random.uniform(own_keys[6], (LEVELS, HEADS, SEQUENCE_TOKENS), jnp.float32) ** level_of(own_keys[6], (LEVELS, HEADS, SEQUENCE_TOKENS), ((1, 2), (2, 64)), -0.2, 0.2)), 0.25, 2.5)
    norm_weight = jnp.clip(1.0 + 0.18 * jax.random.normal(key_list[7], (INNER,), jnp.float32), 0.1, 1.9)
    return dict(mixer_input=mixer_input, gate_input=gate_input, input_proj=input_proj, output_proj=output_proj, step_size=step_size, decay_log=decay_log, level_weight=level_weight, norm_weight=norm_weight)


highest = lax.Precision.HIGHEST

def one_head(c_blocks, b_blocks, scores, head_values, head_steps, head_decay, head_weights):
    block_count = SEQUENCE_TOKENS // BLOCK
    within = jnp.cumsum(head_decay.reshape(block_count, BLOCK), axis=1)
    totals = within[:, -1]
    run_total = jnp.cumsum(totals)
    before = run_total - totals
    step_rows = head_steps.reshape(block_count, BLOCK)
    weights = head_weights.reshape(LEVELS, block_count, BLOCK)
    values = head_values.reshape(block_count, BLOCK, HEADDIM).astype(jnp.float32)
    causal = jnp.arange(BLOCK)[:, None] >= jnp.arange(BLOCK)[None, :]
    log_gap = within[:, :, None] - within[:, None, :]
    decay_mat = jnp.where(causal, jnp.exp(jnp.where(causal, log_gap, 0.0)), 0.0)
    mixing = lax.optimization_barrier((weights[0][:, :, None] * decay_mat * scores * step_rows[:, None, :]).astype(jnp.bfloat16))
    output = jnp.einsum('kqs,ksp->kqp', mixing.astype(jnp.float32), values, precision=highest)
    carry_in = jnp.exp(totals[:, None] - within) * step_rows
    scaled = lax.optimization_barrier((carry_in[:, :, None] * values).astype(jnp.bfloat16))
    states = jnp.einsum('kqp,kqn->kpn', scaled.astype(jnp.float32), b_blocks, precision=highest)
    c_index = jnp.arange(block_count, dtype=jnp.int32)
    for level_index in range(1, LEVELS):
        span_size = 2 ** (level_index - 1)
        grouped = states.reshape(block_count // span_size, span_size, HEADDIM, STATE)
        block_ends = run_total.reshape(block_count // span_size, span_size)
        fold_decay = jnp.exp(block_ends[:, -1:] - block_ends)
        sibling = jnp.einsum('bj,bjpn->bpn', fold_decay, grouped, precision=highest)
        lower_group = c_index // (2 * span_size) * 2
        last_index = lower_group * span_size + span_size - 1
        upper_half = c_index // span_size % 2 == 1
        gap_level = before - run_total[last_index]
        factor = jnp.where(upper_half, jnp.exp(jnp.where(upper_half, gap_level, 0.0)), 0.0)
        bucket = factor[:, None, None] * sibling[lower_group]
        reached = jnp.einsum('kqn,kpn->kqp', c_blocks, bucket, precision=highest)
        output = output + (weights[level_index] * jnp.exp(within))[:, :, None] * reached
    return output.reshape(SEQUENCE_TOKENS, HEADDIM)

def reference(mixer_input, gate_input, input_proj, output_proj, step_size, decay_log, level_weight, norm_weight):
    block_count = SEQUENCE_TOKENS // BLOCK
    c_blocks = output_proj.astype(jnp.float32).reshape(block_count, BLOCK, STATE)
    b_blocks = input_proj.astype(jnp.float32).reshape(block_count, BLOCK, STATE)
    scores = jnp.einsum('kqn,ksn->kqs', c_blocks, b_blocks, precision=highest)
    head_values = jnp.transpose(mixer_input.reshape(SEQUENCE_TOKENS, HEADS, HEADDIM), (1, 0, 2))
    head_weights = jnp.transpose(level_weight, (1, 0, 2))

    def per_head(pieces):
        return one_head(c_blocks, b_blocks, scores, pieces[0], pieces[1], pieces[2], pieces[3])
    outputs = lax.map(per_head, (head_values, step_size, decay_log, head_weights))
    mixed_rows = jnp.transpose(outputs, (1, 0, 2)).reshape(SEQUENCE_TOKENS, HEADS * HEADDIM)
    gated_rows = (mixed_rows * jax.nn.silu(gate_input.astype(jnp.float32))).astype(jnp.bfloat16)
    gated_wide = gated_rows.astype(jnp.float32)
    mean_square = lax.optimization_barrier(jnp.mean(gated_wide * gated_wide, axis=1))
    return (gated_wide * lax.rsqrt(mean_square + 1e-05)[:, None] * norm_weight[None, :]).astype(jnp.bfloat16)
```

```python
import jax
import jax.numpy as jnp
from jax import lax
from jax.experimental import pallas as pl
from jax.experimental.pallas import tpu as pltpu
from jax.sharding import PartitionSpec as P

ROWS, GROUPS, PLACES = 4, 4, 4
BLOCK = 128
STATE = 128
HEADDIM = 64
HEADS = 40
COLS = HEADS * HEADDIM
PART_HEADS = HEADS // PLACES
PART = COLS // PLACES
TILES = PART // 128
BODY = TILES * STATE
META = 16
MSG = BODY + META
LEVELS = 6
f32, bf16, i32 = jnp.float32, jnp.bfloat16, jnp.int32
VMEM = 24 * 2**20


def dot(a, b):
    return jnp.dot(a, b, preferred_element_type=f32)


def three(v):
    hi = v.astype(bf16)
    rest = v - hi.astype(f32)
    mid = rest.astype(bf16)
    return hi, mid, (rest - mid.astype(f32)).astype(bf16)


def iota(shape, dim):
    return lax.broadcasted_iota(i32, shape, dim)


def ones_where(cond):
    return jnp.where(cond, 1.0, 0.0).astype(bf16)


def row_mod(rows, period, shape):
    r = iota(shape, 0)
    turn = jnp.zeros(shape, i32)
    for k in range(period, rows, period):
        turn = turn + jnp.where(r >= k, 1, 0)
    return r - turn * period, turn


def state_kernel(x_ref, b_ref, decay_ref, step_ref, msg_ref, within_ref):
    upper = ones_where(iota((128, 128), 0) <= iota((128, 128), 1))
    within = sum(dot(p, upper) for p in three(decay_ref[...]))
    within_ref[...] = within
    total = within[:, 127:128]
    carry = jnp.exp(total - within) * step_ref[...]
    pad = jnp.zeros((8, 128), f32)

    def stacked(v):
        return jnp.concatenate([p.astype(f32) for p in three(v)] + [pad], axis=0).T

    carry_t = stacked(carry).astype(bf16)
    last = stacked(within)[127:128, :]
    b_t = b_ref[...].astype(f32).T.astype(bf16)
    head, term = row_mod(120, HEADS, (128, 128))
    term = jnp.where(iota((128, 128), 0) >= 120, 7, term)
    side = jnp.where(iota((128, 128), 1) >= HEADDIM, 1, 0)
    lane_term = jnp.where(iota((META, 128), 1) >= 80, 2, jnp.where(iota((META, 128), 1) >= 40, 1, 0))
    meta_row = iota((META, 128), 0)
    for part in range(PLACES):
        meta = jnp.zeros((META, 128), f32)
        for tile in range(TILES):
            pair = part * TILES + tile
            spread = ones_where(jnp.logical_and(head == 2 * pair + side, term < 3))
            cols = slice(pair * 128, (pair + 1) * 128)
            scaled = (dot(carry_t, spread) * x_ref[:, cols].astype(f32)).astype(bf16)
            msg_ref[part, tile * STATE : (tile + 1) * STATE, :] = dot(b_t, scaled).astype(bf16)
            pick = jnp.where(meta_row == 3 * tile + lane_term, last, 0.0).astype(bf16)
            meta = meta + dot(pick, spread)
        msg_ref[part, BODY:MSG, :] = meta.astype(bf16)


def coef_kernel(weight_ref, within_ref, coef_ref):
    grown = jnp.exp(within_ref[...])
    rows = [weight_ref[level] * grown for level in range(1, LEVELS + 1)]
    stack = jnp.concatenate(rows + [jnp.zeros((16, 128), f32)], axis=0).T
    hi, lo, _ = three(stack)
    shape = (256, 128)
    head, level = row_mod(240, HEADS, shape)
    level = jnp.where(iota(shape, 0) >= 240, 99, level)
    lane = iota(shape, 1)
    for part in range(PLACES):
        own = head - part * PART_HEADS
        ok = jnp.logical_and(jnp.logical_and(own >= 0, own < PART_HEADS), level < LEVELS)
        target = jnp.where(ok, level * PART_HEADS + own, 999)
        packed = dot(hi, ones_where(lane == target)) + dot(lo, ones_where(lane == target + 64))
        coef_ref[part] = packed.astype(bf16)


def local_kernel(x_ref, b_ref, c_ref, step_ref, weight_ref, within_ref, out_ref):
    scores = lax.dot_general(
        c_ref[...], b_ref[...], (((1,), (1,)), ((), ())), preferred_element_type=f32
    )
    scores = jnp.where(iota((128, 128), 0) >= iota((128, 128), 1), scores, 0.0)
    pad = jnp.zeros((128 - HEADS, 128), f32)
    within = within_ref[...]
    within_t = jnp.concatenate([within, pad], axis=0).T
    weight_t = jnp.concatenate([weight_ref[0], pad], axis=0).T
    step = step_ref[...]
    left = iota((128, 128), 1) < HEADDIM
    zero = jnp.zeros((128, 128), bf16)

    def mixing(h):
        gap = jnp.minimum(within_t[:, h : h + 1] - within[h : h + 1, :], 0.0)
        gain = weight_t[:, h : h + 1] * jnp.exp(gap)
        return (gain * scores * step[h : h + 1, :]).astype(bf16)

    for pair in range(HEADS // 2):
        cols = slice(pair * 128, (pair + 1) * 128)
        x = x_ref[:, cols]
        both = jnp.concatenate([mixing(2 * pair), mixing(2 * pair + 1)], axis=1)
        sides = jnp.concatenate([jnp.where(left, x, zero), jnp.where(left, zero, x)], axis=0)
        out_ref[:, cols] = dot(both, sides)


def total_of(meta, tile):
    return meta[3 * tile : 3 * tile + 1] + meta[3 * tile + 1 : 3 * tile + 2] + meta[3 * tile + 2 : 3 * tile + 3]


def put_total(meta, tile, total):
    row = iota((META, 128), 0)
    for k, p in enumerate(three(total)):
        meta = jnp.where(row == 3 * tile + k, p.astype(f32), meta)
    return meta


def group_kernel(parts_ref, out_ref):
    metas = [parts_ref[j, BODY:MSG, :].astype(f32) for j in range(PLACES)]
    meta = jnp.zeros((META, 128), f32)
    for tile in range(TILES):
        rows = slice(tile * STATE, (tile + 1) * STATE)
        t = [total_of(m, tile) for m in metas]
        s = [parts_ref[j, rows, :].astype(f32) for j in range(PLACES)]
        acc = s[0]
        for j in range(1, PLACES):
            acc = jnp.exp(t[j]) * acc + s[j]
        out_ref[rows, :] = acc.astype(bf16)
        meta = put_total(meta, tile, t[0] + t[1] + t[2] + t[3])
    out_ref[BODY:MSG, :] = meta.astype(bf16)


def flag(cond):
    return jnp.where(cond, 1.0, 0.0).astype(f32)


def row_kernel(place_ref, own_ref, one_ref, two_ref, three_ref, out_ref):
    group = place_ref[0]
    refs = (own_ref, one_ref, two_ref, three_ref)
    spot = [(group + 4 - k) % 4 for k in range(GROUPS)]
    metas = [r[BODY:MSG, :].astype(f32) for r in refs]
    meta = jnp.zeros((META, 128), f32)
    for tile in range(TILES):
        rows = slice(tile * STATE, (tile + 1) * STATE)
        t = [total_of(m, tile) for m in metas]
        acc = None
        for k in range(GROUPS):
            gap = sum(t[j] * flag(spot[j] > spot[k]) for j in range(GROUPS) if j != k)
            term = jnp.exp(gap) * refs[k][rows, :].astype(f32)
            acc = term if acc is None else acc + term
        out_ref[rows, :] = acc.astype(bf16)
        meta = put_total(meta, tile, t[0] + t[1] + t[2] + t[3])
    out_ref[BODY:MSG, :] = meta.astype(bf16)


def reach_kernel(
    place_ref, c_ref, coef_ref, parts_ref, g1_ref, g2_ref, g3_ref, r1_ref, r2_ref, r3_ref, out_ref
):
    group, row = place_ref[0], place_ref[1]
    part_metas = [parts_ref[j, BODY:MSG, :].astype(f32) for j in range(PLACES)]
    group_refs = (g1_ref, g2_ref, g3_ref)
    row_refs = (r1_ref, r2_ref, r3_ref)
    group_metas = [r[BODY:MSG, :].astype(f32) for r in group_refs]
    row_metas = [r[BODY:MSG, :].astype(f32) for r in row_refs]

    def buckets(index, refs, t, rows):
        vals = [r[rows, :].astype(f32) for r in refs]
        near = flag(index % 2 == 1) * vals[0]
        w1 = flag(index == 2)
        w2 = flag(index >= 2) * jnp.exp(t[0])
        w3 = flag(index == 3) * jnp.exp(t[0] + t[1])
        far = w1 * vals[0] + w2 * vals[1] + w3 * vals[2]
        return near, far

    def split(v):
        hi = v.astype(bf16)
        return jnp.concatenate([hi, (v - hi.astype(f32)).astype(bf16)], axis=0)

    slot = iota((128, 128), 0)
    slot = jnp.where(slot >= 64, slot - 64, slot)
    side = jnp.where(iota((128, 128), 1) >= HEADDIM, 1, 0)
    for first in range(0, TILES, 2):
        tiles = range(first, min(first + 2, TILES))
        low_b, mid_b, high_b = [], [], []
        group_b = [[], [], [], []]
        offs, skip = [[], [], [], []], []
        for tile in tiles:
            rows = slice(tile * STATE, (tile + 1) * STATE)
            t = [total_of(m, tile) for m in part_metas]
            s0, s1 = parts_ref[0, rows, :], parts_ref[1, rows, :]
            low_b.append(s0)
            mid_b.append(split(jnp.exp(t[1]) * s0.astype(f32) + s1.astype(f32)))
            high_b.append(parts_ref[2, rows, :])
            tg = [total_of(m, tile) for m in group_metas]
            tr = [total_of(m, tile) for m in row_metas]
            b3, b4 = buckets(group, group_refs, tg, rows)
            b5, b6 = buckets(row, row_refs, tr, rows)
            lead = jnp.exp(
                flag(group >= 1) * tg[0] + flag(group >= 2) * tg[1] + flag(group >= 3) * tg[2]
            )
            for k, v in enumerate((b3, b4, lead * b5, lead * b6)):
                group_b[k].append(split(v))
            offs[1].append(jnp.exp(t[0]))
            offs[2].append(jnp.exp(t[0] + t[1]))
            offs[3].append(jnp.exp(t[0] + t[1] + t[2]))
            skip.append(jnp.exp(t[2]))

        def wide(pieces):
            return pieces[0] if len(pieces) == 1 else jnp.concatenate(pieces, axis=1)

        spread = [
            wide([ones_where(slot == level * PART_HEADS + 2 * tile + side) for tile in tiles])
            for level in range(LEVELS)
        ]
        low_w, mid_w, high_w = wide(low_b), wide(mid_b), wide(high_b)
        group_w = [wide(v) for v in group_b]
        lanes = slice(first * 128, (first + len(tiles)) * 128)
        for place in range(PLACES):
            c = c_ref[place]
            cc = jnp.concatenate([c, c], axis=1)
            coef = coef_ref[place]
            acc = None
            for k in range(4):
                term = dot(coef, spread[2 + k]) * dot(cc, group_w[k])
                acc = term if acc is None else acc + term
            if place:
                acc = acc * wide(offs[place])
            if place == 1:
                acc = acc + dot(coef, spread[0]) * dot(c, low_w)
            if place == 3:
                acc = acc + dot(coef, spread[0]) * dot(c, high_w)
            if place >= 2:
                term = dot(coef, spread[1]) * dot(cc, mid_w)
                acc = acc + (term * wide(skip) if place == 3 else term)
            out_ref[place, :, lanes] = acc.astype(bf16)


def gate_kernel(local_ref, reached_ref, gate_ref, gated_ref, square_ref):
    acc = jnp.zeros((128, 128), f32)
    for pair in range(HEADS // 2):
        cols = slice(pair * 128, (pair + 1) * 128)
        part, tile = pair // TILES, pair % TILES
        mixed = local_ref[:, cols] + reached_ref[part, :, tile * 128 : (tile + 1) * 128].astype(f32)
        gate = gate_ref[:, cols].astype(f32)
        gated = (mixed * (gate / (1.0 + jnp.exp(-gate)))).astype(bf16)
        gated_ref[:, cols] = gated
        wide = gated.astype(f32)
        acc = acc + wide * wide
    square_ref[...] = acc


def norm_kernel(gated_ref, own_ref, other_ref, weight_ref, out_ref):
    mean = jnp.sum(own_ref[...] + other_ref[...], axis=1, keepdims=True) / (2.0 * COLS)
    inverse = lax.rsqrt(mean + 1e-05)
    for pair in range(HEADS // 2):
        cols = slice(pair * 128, (pair + 1) * 128)
        out_ref[:, cols] = (
            gated_ref[:, cols].astype(f32) * inverse * weight_ref[:, cols]
        ).astype(bf16)


def call(kernel, name, outs, *args, smem=0, flops=10**8, size=4 * 10**6):
    specs = [pl.BlockSpec(memory_space=pltpu.SMEM)] * smem
    specs += [pl.BlockSpec(memory_space=pltpu.VMEM)] * (len(args) - smem)
    many = isinstance(outs, list)
    shapes = [jax.ShapeDtypeStruct(*o) for o in outs] if many else jax.ShapeDtypeStruct(*outs)
    return kernel_call(kernel, name, specs, shapes, flops, size)(*args)


def kernel_call(kernel, name, specs, shapes, flops, size):
    many = isinstance(shapes, list)
    out_specs = pl.BlockSpec(memory_space=pltpu.VMEM)
    return pl.pallas_call(
        kernel,
        name=name,
        in_specs=specs,
        out_specs=[out_specs] * len(shapes) if many else out_specs,
        out_shape=shapes,
        cost_estimate=pl.CostEstimate(flops=flops, bytes_accessed=size, transcendentals=0),
        compiler_params=pltpu.CompilerParams(vmem_limit_bytes=VMEM),
    )


def spot_of(index):
    return index // 16, index // 4 % 4, index % 4


def index_of(row, group, place):
    return row * 16 + group * 4 + place


def along_groups(value, shift):
    pairs = []
    for index in range(ROWS * GROUPS * PLACES):
        row, group, place = spot_of(index)
        pairs.append((index, index_of(row, (group + shift) % GROUPS, place)))
    return lax.ppermute(value, "ctx", pairs)


def along_rows(value, shift):
    pairs = []
    for index in range(ROWS * GROUPS * PLACES):
        row, group, place = spot_of(index)
        if row + shift < ROWS:
            pairs.append((index, index_of(row + shift, group, place)))
    return lax.ppermute(value, "ctx", pairs)


def on_device(
    mixer_input,
    gate_input,
    input_proj,
    output_proj,
    step_size,
    decay_log,
    level_weight,
    norm_weight,
):
    position = lax.axis_index("ctx")
    place = jnp.stack([position // 4 % 4, position // 16]).astype(i32)
    lines = [
        [index_of(row, group, p) for p in range(PLACES)]
        for row in range(ROWS)
        for group in range(GROUPS)
    ]

    def within_line(value):
        return lax.all_to_all(value, "ctx", 0, 0, axis_index_groups=lines)

    states, within = call(
        state_kernel,
        "block_states",
        [((PLACES, MSG, 128), bf16), ((HEADS, 128), f32)],
        mixer_input,
        input_proj,
        decay_log,
        step_size,
    )
    coefs = call(coef_kernel, "level_gains", ((PLACES, 128, 128), bf16), level_weight, within)
    c_all = jnp.broadcast_to(output_proj[None], (PLACES, 128, 128))
    parts = within_line(states)
    side = within_line(jnp.concatenate([c_all, coefs], axis=1))
    local = call(
        local_kernel,
        "local_part",
        ((128, COLS), f32),
        mixer_input,
        input_proj,
        output_proj,
        step_size,
        level_weight,
        within,
        flops=10**10,
        size=10**7,
    )
    group = call(group_kernel, "group_state", ((MSG, 128), bf16), parts)
    others = [along_groups(group, k) for k in (1, 2, 3)]
    total = call(row_kernel, "row_state", ((MSG, 128), bf16), place, group, *others, smem=1)
    rows = [along_rows(total, k) for k in (1, 2, 3)]
    reached = call(
        reach_kernel,
        "level_outputs",
        ((PLACES, 128, PART), bf16),
        place,
        side[:, :128],
        side[:, 128:],
        parts,
        *others,
        *rows,
        smem=1,
    )
    back = within_line(reached)
    gated, square = call(
        gate_kernel, "gate", [((128, COLS), bf16), ((128, 128), f32)], local, back, gate_input
    )
    other = lax.ppermute(square, "head", [(0, 1), (1, 0)])
    return call(
        norm_kernel, "norm", ((128, COLS), bf16), gated, square, other, norm_weight.reshape(1, COLS)
    )


def solution(mesh):
    in_specs = (
        P(("seq", "ctx"), "head"),
        P(("seq", "ctx"), "head"),
        P(("seq", "ctx"), None),
        P(("seq", "ctx"), None),
        P("head", ("seq", "ctx")),
        P("head", ("seq", "ctx")),
        P(None, "head", ("seq", "ctx")),
        P("head"),
    )
    out_specs = P(("seq", "ctx"), "head")
    return jax.shard_map(
        on_device, mesh=mesh, in_specs=in_specs, out_specs=out_specs, check_vma=False
    )
```

```python
import jax
import jax.numpy as jnp
from jax import lax
from jax.experimental import pallas as pl
from jax.experimental.pallas import tpu as pltpu
from jax.sharding import PartitionSpec as P

ROWS, GROUPS, PLACES = 4, 4, 4
BLOCK = 128
STATE = 128
HEADDIM = 64
HEADS = 40
COLS = HEADS * HEADDIM
PART_HEADS = HEADS // PLACES
PART = COLS // PLACES
TILES = PART // 128
BODY = TILES * STATE
HALF = BODY // 2
META = 16
SIDE = BODY + META
LEVELS = 6
f32, bf16, i32 = jnp.float32, jnp.bfloat16, jnp.int32
VMEM = 24 * 2**20


def dot(a, b):
    return jnp.dot(a, b, preferred_element_type=f32)


def three(v):
    hi = v.astype(bf16)
    rest = v - hi.astype(f32)
    mid = rest.astype(bf16)
    return hi, mid, (rest - mid.astype(f32)).astype(bf16)


def iota(shape, dim):
    return lax.broadcasted_iota(i32, shape, dim)


def ones_where(cond):
    return jnp.where(cond, 1.0, 0.0).astype(bf16)


def row_mod(rows, period, shape):
    r = iota(shape, 0)
    turn = jnp.zeros(shape, i32)
    for k in range(period, rows, period):
        turn = turn + jnp.where(r >= k, 1, 0)
    return r - turn * period, turn


def worker_message(part, x, carry_t, last, b_t, msg_ref):
    head, _ = row_mod(120, HEADS, (128, 128))
    head = jnp.where(iota((128, 128), 0) >= 120, 999, head)
    side = jnp.where(iota((128, 128), 1) >= HEADDIM, 1, 0)
    lane = iota((META, 128), 1)
    lane_term = jnp.where(lane >= 2 * HEADS, 2, jnp.where(lane >= HEADS, 1, 0))
    meta_row = iota((META, 128), 0)
    base = part * PART_HEADS
    spread = [ones_where(head == base + 2 * k + side) for k in range(TILES)]
    scaled = (dot(carry_t, jnp.concatenate(spread, axis=1)) * x.astype(f32)).astype(bf16)
    state = dot(b_t, scaled).astype(bf16)
    meta = jnp.zeros((META, 128), f32)
    for k in range(TILES):
        msg_ref[part, k * STATE : (k + 1) * STATE, :] = state[:, k * 128 : (k + 1) * 128]
        pick = jnp.where(meta_row == 3 * k + lane_term, last, 0.0).astype(bf16)
        meta = meta + dot(pick, spread[k])
    msg_ref[part, BODY:SIDE, :] = meta.astype(bf16)


def state_kernel(
    x_ref, b_ref, c_ref, decay_ref, step_ref, weight_ref, msg_ref, within_ref,
    x_buf, b_buf, c_buf, decay_buf, step_buf, weight_buf, sems,
):
    copies = [
        pltpu.make_async_copy(decay_ref, decay_buf, sems.at[0]),
        pltpu.make_async_copy(step_ref, step_buf, sems.at[1]),
        pltpu.make_async_copy(b_ref, b_buf, sems.at[2]),
    ]
    for part in range(PLACES):
        cols = pl.ds(part * PART, PART)
        copies.append(pltpu.make_async_copy(x_ref.at[:, cols], x_buf.at[part], sems.at[3 + part]))
    copies.append(pltpu.make_async_copy(weight_ref, weight_buf, sems.at[7]))
    copies.append(pltpu.make_async_copy(c_ref, c_buf, sems.at[8]))
    for c in copies:
        c.start()
    upper = ones_where(iota((128, 128), 0) <= iota((128, 128), 1))
    copies[0].wait()
    within = sum(dot(p, upper) for p in three(decay_buf[...]))
    within_ref[...] = within
    total = within[:, 127:128]
    copies[1].wait()
    carry = jnp.exp(total - within) * step_buf[...]
    pad = jnp.zeros((8, 128), f32)

    def stacked(v):
        return jnp.concatenate([p.astype(f32) for p in three(v)] + [pad], axis=0).T

    carry_t = stacked(carry).astype(bf16)
    last = stacked(within)[127:128, :]
    copies[2].wait()
    b_t = b_buf[...].astype(f32).T.astype(bf16)
    for part in range(PLACES):
        copies[3 + part].wait()
        worker_message(part, x_buf[part], carry_t, last, b_t, msg_ref)
    copies[7].wait()
    copies[8].wait()
    gains = level_gains(weight_buf, within)
    for part in range(PLACES):
        msg_ref[part, SIDE : SIDE + 128, :] = c_buf[...]
        msg_ref[part, SIDE + 128 :, :] = gains[part]


def level_gains(weights, within):
    grown = jnp.exp(within)
    rows = [weights[level] * grown for level in range(1, LEVELS + 1)]
    stack = jnp.concatenate(rows + [jnp.zeros((16, 128), f32)], axis=0).T
    hi, lo, _ = three(stack)
    shape = (256, 128)
    head, level = row_mod(240, HEADS, shape)
    level = jnp.where(iota(shape, 0) >= 240, 99, level)
    lane = iota(shape, 1)
    gains = []
    for part in range(PLACES):
        own = head - part * PART_HEADS
        ok = jnp.logical_and(jnp.logical_and(own >= 0, own < PART_HEADS), level < LEVELS)
        target = jnp.where(ok, level * PART_HEADS + own, 999)
        packed = dot(hi, ones_where(lane == target)) + dot(lo, ones_where(lane == target + 64))
        gains.append(packed.astype(bf16))
    return gains


def local_kernel(x_ref, b_ref, c_ref, step_ref, weight_ref, within_ref, out_ref):
    scores = lax.dot_general(
        c_ref[...], b_ref[...], (((1,), (1,)), ((), ())), preferred_element_type=f32
    )
    scores = jnp.where(iota((128, 128), 0) >= iota((128, 128), 1), scores, 0.0)
    pad = jnp.zeros((128 - HEADS, 128), f32)
    within = within_ref[...]
    within_t = jnp.concatenate([within, pad], axis=0).T
    weight_t = jnp.concatenate([weight_ref[0], pad], axis=0).T
    step = step_ref[...]
    left = iota((128, 128), 1) < HEADDIM
    zero = jnp.zeros((128, 128), bf16)

    def mixing(h):
        gap = jnp.minimum(within_t[:, h : h + 1] - within[h : h + 1, :], 0.0)
        gain = weight_t[:, h : h + 1] * jnp.exp(gap)
        return (gain * scores * step[h : h + 1, :]).astype(bf16)

    for pair in range(HEADS // 2):
        cols = slice(pair * 128, (pair + 1) * 128)
        x = x_ref[:, cols]
        both = jnp.concatenate([mixing(2 * pair), mixing(2 * pair + 1)], axis=1)
        sides = jnp.concatenate([jnp.where(left, x, zero), jnp.where(left, zero, x)], axis=0)
        out_ref[:, cols] = dot(both, sides)


def total_of(meta, tile):
    return meta[3 * tile : 3 * tile + 1] + meta[3 * tile + 1 : 3 * tile + 2] + meta[3 * tile + 2 : 3 * tile + 3]


def put_total(meta, tile, total):
    row = iota((META, 128), 0)
    for k, p in enumerate(three(total)):
        meta = jnp.where(row == 3 * tile + k, p.astype(f32), meta)
    return meta


def tile_rows(tile):
    return slice(tile * STATE, (tile + 1) * STATE)


def group_kernel(parts_ref, out_ref):
    metas = [parts_ref[j, BODY:SIDE, :].astype(f32) for j in range(PLACES)]
    meta = jnp.zeros((META, 128), f32)
    for tile in range(TILES):
        rows = tile_rows(tile)
        t = [total_of(m, tile) for m in metas]
        acc = parts_ref[0, rows, :].astype(f32)
        for j in range(1, PLACES):
            acc = jnp.exp(t[j]) * acc + parts_ref[j, rows, :].astype(f32)
        out_ref[rows, :] = acc.astype(bf16)
        meta = put_total(meta, tile, t[0] + t[1] + t[2] + t[3])
    out_ref[BODY:, :] = meta.astype(bf16)


def flag(cond):
    return jnp.where(cond, 1.0, 0.0).astype(f32)


def opposite_tile(top_ref, low_ref, tile):
    start, end = tile * STATE, (tile + 1) * STATE
    if end <= HALF:
        return top_ref[start:end, :].astype(f32)
    if start >= HALF:
        return low_ref[start - HALF : end - HALF, :].astype(f32)
    pieces = [top_ref[start:HALF, :], low_ref[: end - HALF, :]]
    return jnp.concatenate([p.astype(f32) for p in pieces], axis=0)


def group_tiles(g1_ref, top_ref, low_ref, g3_ref, tile):
    rows = tile_rows(tile)
    return (
        g1_ref[rows, :].astype(f32),
        opposite_tile(top_ref, low_ref, tile),
        g3_ref[rows, :].astype(f32),
    )


def group_totals(g1_ref, low_ref, g3_ref):
    return [
        g1_ref[BODY:, :].astype(f32),
        low_ref[BODY - HALF :, :].astype(f32),
        g3_ref[BODY:, :].astype(f32),
    ]


def row_kernel(place_ref, own_ref, g1_ref, top_ref, low_ref, g3_ref, out_ref):
    spot = [(place_ref[0] + GROUPS - k) % GROUPS for k in range(GROUPS)]
    metas = [own_ref[BODY:, :].astype(f32)] + group_totals(g1_ref, low_ref, g3_ref)
    meta = jnp.zeros((META, 128), f32)
    for tile in range(TILES):
        rows = tile_rows(tile)
        t = [total_of(m, tile) for m in metas]
        values = (own_ref[rows, :].astype(f32),) + group_tiles(g1_ref, top_ref, low_ref, g3_ref, tile)
        acc = None
        for k in range(GROUPS):
            gap = sum(t[j] * flag(spot[j] > spot[k]) for j in range(GROUPS) if j != k)
            term = jnp.exp(gap) * values[k]
            acc = term if acc is None else acc + term
        out_ref[rows, :] = acc.astype(bf16)
        meta = put_total(meta, tile, t[0] + t[1] + t[2] + t[3])
    out_ref[BODY:, :] = meta.astype(bf16)


def split(v):
    hi = v.astype(bf16)
    return jnp.concatenate([hi, (v - hi.astype(f32)).astype(bf16)], axis=0)


def wide(pieces):
    return pieces[0] if len(pieces) == 1 else jnp.concatenate(pieces, axis=1)


def gain_spread(tiles, level):
    slot = iota((128, 128), 0)
    slot = jnp.where(slot >= 64, slot - 64, slot)
    side = jnp.where(iota((128, 128), 1) >= HEADDIM, 1, 0)
    return wide(
        [ones_where(slot == level * PART_HEADS + 2 * tile + side) for tile in tiles]
    )


def token_side(parts_ref, place):
    c, coef = parts_ref[place, SIDE : SIDE + 128, :], parts_ref[place, SIDE + 128 :, :]
    return c, jnp.concatenate([c, c], axis=1), coef


def block_lead(metas, place, tiles):
    return wide(
        [jnp.exp(sum(total_of(m, tile) for m in metas[:place])) for tile in tiles]
    )


def near_kernel(place_ref, parts_ref, g1_ref, top_ref, low_ref, g3_ref, out_ref):
    group = place_ref[0]
    part_metas = [parts_ref[j, BODY:SIDE, :].astype(f32) for j in range(PLACES)]
    metas = group_totals(g1_ref, low_ref, g3_ref)
    odd, upper = flag(group % 2 == 1), flag(group >= 2)
    second, third = flag(group == 2), flag(group == 3)
    for start in range(0, TILES, 2):
        tiles = range(start, min(start + 2, TILES))
        low_b, mid_b, high_b, b3, b4, skip = [], [], [], [], [], []
        for tile in tiles:
            rows = tile_rows(tile)
            t = [total_of(m, tile) for m in part_metas]
            s0, s1 = parts_ref[0, rows, :], parts_ref[1, rows, :]
            low_b.append(s0)
            mid_b.append(split(jnp.exp(t[1]) * s0.astype(f32) + s1.astype(f32)))
            high_b.append(parts_ref[2, rows, :])
            skip.append(jnp.exp(t[2]))
            t1, t2 = total_of(metas[0], tile), total_of(metas[1], tile)
            v1, v2, v3 = group_tiles(g1_ref, top_ref, low_ref, g3_ref, tile)
            b3.append(split(odd * v1))
            w2, w3 = upper * jnp.exp(t1), third * jnp.exp(t1 + t2)
            b4.append(split(second * v1 + w2 * v2 + w3 * v3))
        spread = [gain_spread(tiles, level) for level in range(4)]
        low_w, mid_w, high_w = wide(low_b), wide(mid_b), wide(high_b)
        b3_w, b4_w = wide(b3), wide(b4)
        lanes = slice(start * 128, (start + len(tiles)) * 128)
        for place in range(PLACES):
            c, cc, coef = token_side(parts_ref, place)
            acc = dot(coef, spread[2]) * dot(cc, b3_w) + dot(coef, spread[3]) * dot(cc, b4_w)
            if place:
                acc = acc * block_lead(part_metas, place, tiles)
            if place == 1:
                acc = acc + dot(coef, spread[0]) * dot(c, low_w)
            if place == 3:
                acc = acc + dot(coef, spread[0]) * dot(c, high_w)
            if place >= 2:
                term = dot(coef, spread[1]) * dot(cc, mid_w)
                acc = acc + (term * wide(skip) if place == 3 else term)
            out_ref[place, :, lanes] = acc


def far_kernel(
    place_ref, parts_ref, g1_ref, low_ref, g3_ref, r1_ref, r2_ref, r3_ref, near_ref, out_ref
):
    group, row = place_ref[0], place_ref[1]
    part_metas = [parts_ref[j, BODY:SIDE, :].astype(f32) for j in range(PLACES)]
    metas = group_totals(g1_ref, low_ref, g3_ref)
    row_metas = [r[BODY:, :].astype(f32) for r in (r1_ref, r2_ref)]
    odd, upper = flag(row % 2 == 1), flag(row >= 2)
    second, third = flag(row == 2), flag(row == 3)
    for start in range(0, TILES, 2):
        tiles = range(start, min(start + 2, TILES))
        b5, b6 = [], []
        for tile in tiles:
            rows = tile_rows(tile)
            t = [total_of(m, tile) for m in metas]
            t1, t2 = (total_of(m, tile) for m in row_metas)
            lead = jnp.exp(sum(flag(group > k) * t[k] for k in range(3)))
            v1, v2, v3 = (r[rows, :].astype(f32) for r in (r1_ref, r2_ref, r3_ref))
            b5.append(split((lead * odd) * v1))
            w2, w3 = lead * upper * jnp.exp(t1), lead * third * jnp.exp(t1 + t2)
            b6.append(split((lead * second) * v1 + w2 * v2 + w3 * v3))
        spread = [gain_spread(tiles, level) for level in (4, 5)]
        b5_w, b6_w = wide(b5), wide(b6)
        lanes = slice(start * 128, (start + len(tiles)) * 128)
        for place in range(PLACES):
            _, cc, coef = token_side(parts_ref, place)
            acc = dot(coef, spread[0]) * dot(cc, b5_w) + dot(coef, spread[1]) * dot(cc, b6_w)
            if place:
                acc = acc * block_lead(part_metas, place, tiles)
            out_ref[place, :, lanes] = (acc + near_ref[place, :, lanes]).astype(bf16)


def gate_kernel(local_ref, reached_ref, gate_ref, gated_ref, square_ref):
    acc = jnp.zeros((128, 128), f32)
    for pair in range(HEADS // 2):
        cols = slice(pair * 128, (pair + 1) * 128)
        part, tile = pair // TILES, pair % TILES
        mixed = local_ref[:, cols] + reached_ref[part, :, tile * 128 : (tile + 1) * 128].astype(f32)
        gate = gate_ref[:, cols].astype(f32)
        gated = (mixed * (gate / (1.0 + jnp.exp(-gate)))).astype(bf16)
        gated_ref[:, cols] = gated
        wide = gated.astype(f32)
        acc = acc + wide * wide
    square_ref[...] = acc


def norm_kernel(gated_ref, own_ref, other_ref, weight_ref, out_ref):
    mean = jnp.sum(own_ref[...] + other_ref[...], axis=1, keepdims=True) / (2.0 * COLS)
    inverse = jnp.broadcast_to(lax.rsqrt(mean + 1e-05), (128, 128))
    for pair in range(HEADS // 2):
        cols = slice(pair * 128, (pair + 1) * 128)
        out_ref[:, cols] = (
            gated_ref[:, cols].astype(f32) * inverse * weight_ref[:, cols]
        ).astype(bf16)


def call(
    kernel, name, outs, *args, smem=0, far=0, scratch=(), flops=10**8, size=4 * 10**6, vmem=VMEM
):
    whole = pl.BlockSpec(memory_space=pltpu.VMEM)
    specs = [pl.BlockSpec(memory_space=pltpu.SMEM)] * smem
    specs += [pl.BlockSpec(memory_space=pl.ANY)] * far
    specs += [whole] * (len(args) - smem - far)
    return pl.pallas_call(
        kernel,
        name=name,
        in_specs=specs,
        out_specs=[whole] * len(outs),
        out_shape=[jax.ShapeDtypeStruct(*o) for o in outs],
        scratch_shapes=list(scratch),
        cost_estimate=pl.CostEstimate(flops=flops, bytes_accessed=size, transcendentals=0),
        compiler_params=pltpu.CompilerParams(vmem_limit_bytes=vmem),
    )(*args)


def spot_of(index):
    return index // 16, index // 4 % 4, index % 4


def index_of(row, group, place):
    return row * 16 + group * 4 + place


def to_group(value, shift):
    pairs = []
    for index in range(ROWS * GROUPS * PLACES):
        row, group, place = spot_of(index)
        pairs.append((index, index_of(row, (group + shift) % GROUPS, place)))
    return lax.ppermute(value, "ctx", pairs)


def to_row(value, shift):
    pairs = []
    for index in range(ROWS * GROUPS * PLACES):
        row, group, place = spot_of(index)
        if row + shift < ROWS:
            pairs.append((index, index_of(row + shift, group, place)))
    return lax.ppermute(value, "ctx", pairs)


LINES = [[index_of(r, g, p) for p in range(PLACES)] for r in range(ROWS) for g in range(GROUPS)]


def exchange(value, lines):
    return lax.all_to_all(value, "ctx", 0, 0, axis_index_groups=lines)


def on_device(
    mixer_input,
    gate_input,
    input_proj,
    output_proj,
    step_size,
    decay_log,
    level_weight,
    norm_weight,
):
    position = lax.axis_index("ctx")
    group = position // 4 % 4
    place = jnp.stack([group, position // 16]).astype(i32)

    messages, within = call(
        state_kernel,
        "block_states",
        [((PLACES, SIDE + 256, 128), bf16), ((HEADS, 128), f32)],
        mixer_input,
        input_proj,
        output_proj,
        decay_log,
        step_size,
        level_weight,
        far=6,
        vmem=60 * 2**20,
        scratch=[
            pltpu.VMEM((PLACES, 128, PART), bf16),
            pltpu.VMEM((128, 128), bf16),
            pltpu.VMEM((128, 128), bf16),
            pltpu.VMEM((HEADS, 128), f32),
            pltpu.VMEM((HEADS, 128), f32),
            pltpu.VMEM((LEVELS + 1, HEADS, 128), f32),
            pltpu.SemaphoreType.DMA((9,)),
        ],
    )
    (local,) = call(
        local_kernel,
        "local_part",
        [((128, COLS), f32)],
        mixer_input,
        input_proj,
        output_proj,
        step_size,
        level_weight,
        within,
        flops=10**10,
        size=10**7,
    )
    parts = exchange(messages, LINES)
    (own,) = call(group_kernel, "group_state", [((BODY + META, 128), bf16)], parts)
    before, after = to_group(own, 1), to_group(own, 3)
    top, low = to_group(before[:HALF], 1), to_group(after[HALF:], 3)
    groups = (before, top, low, after)
    (total,) = call(
        row_kernel, "row_state", [((BODY + META, 128), bf16)], place, own, *groups, smem=1
    )
    rows = [to_row(total, k) for k in (1, 2, 3)]
    (near,) = call(
        near_kernel,
        "near_levels",
        [((PLACES, 128, PART), f32)],
        place,
        parts,
        *groups,
        smem=1,
        flops=10**10,
    )
    (reached,) = call(
        far_kernel,
        "far_levels",
        [((PLACES, 128, PART), bf16)],
        place,
        parts,
        before,
        low,
        after,
        *rows,
        near,
        smem=1,
    )
    back = exchange(reached, LINES)
    gated, square = call(
        gate_kernel, "gate", [((128, COLS), bf16), ((128, 128), f32)], local, back, gate_input
    )
    other = lax.ppermute(square, "head", [(0, 1), (1, 0)])
    (out,) = call(
        norm_kernel,
        "norm",
        [((128, COLS), bf16)],
        gated,
        square,
        other,
        norm_weight.reshape(1, COLS),
    )
    return out


def solution(mesh):
    in_specs = (
        P(("seq", "ctx"), "head"),
        P(("seq", "ctx"), "head"),
        P(("seq", "ctx"), None),
        P(("seq", "ctx"), None),
        P("head", ("seq", "ctx")),
        P("head", ("seq", "ctx")),
        P(None, "head", ("seq", "ctx")),
        P("head"),
    )
    out_specs = P(("seq", "ctx"), "head")
    return jax.shard_map(
        on_device, mesh=mesh, in_specs=in_specs, out_specs=out_specs, check_vma=False
    )
```

```python
import functools

import jax
import jax.numpy as jnp
from jax import lax
from jax.experimental import pallas as pl
from jax.experimental.pallas import tpu as pltpu
from jax.sharding import PartitionSpec as P

ROWS, GROUPS, PLACES = 4, 4, 4
BLOCK = 128
STATE = 128
HEADDIM = 64
HEADS = 40
COLS = HEADS * HEADDIM
PART_HEADS = HEADS // PLACES
PART = COLS // PLACES
TILES = PART // 128
BODY = TILES * STATE
AHEAD = 3
META = 16
SIDE = BODY + META
KEEP = SIDE + 64
MSG = KEEP + 64
LEVELS = 6
FIRST, SECOND = (2, 3, 1), (0,)
MASKS = FIRST + SECOND
f32, bf16, i32 = jnp.float32, jnp.bfloat16, jnp.int32
VMEM = 24 * 2**20


def spots():
    position = lax.axis_index("ctx")
    return position // 4 % 4, position // 16, position % 4, lax.axis_index("head")


def dot(a, b):
    return jnp.dot(a, b, preferred_element_type=f32)


def three(v):
    hi = v.astype(bf16)
    rest = v - hi.astype(f32)
    mid = rest.astype(bf16)
    return hi, mid, (rest - mid.astype(f32)).astype(bf16)


def iota(shape, dim):
    return lax.broadcasted_iota(i32, shape, dim)


def ones_where(cond):
    return jnp.where(cond, 1.0, 0.0).astype(bf16)


def row_mod(rows, period, shape):
    r = iota(shape, 0)
    turn = jnp.zeros(shape, i32)
    for k in range(period, rows, period):
        turn = turn + jnp.where(r >= k, 1, 0)
    return r - turn * period, turn


def worker_message(part, x, carry_t, last, b_t, gains, c_half, msg_ref):
    head, _ = row_mod(120, HEADS, (128, 128))
    head = jnp.where(iota((128, 128), 0) >= 120, 999, head)
    side = jnp.where(iota((128, 128), 1) >= HEADDIM, 1, 0)
    lane = iota((META, 128), 1)
    lane_term = jnp.where(lane >= 2 * HEADS, 2, jnp.where(lane >= HEADS, 1, 0))
    meta_row = iota((META, 128), 0)
    base = part * PART_HEADS
    spread = [ones_where(head - base == 2 * k + side) for k in range(TILES)]
    scaled = (dot(carry_t, jnp.concatenate(spread, axis=1)) * x.astype(f32)).astype(bf16)
    state = dot(b_t, scaled).astype(bf16)
    meta = jnp.zeros((META, 128), f32)
    for k in range(TILES):
        msg_ref[k * STATE : (k + 1) * STATE, :] = state[:, k * 128 : (k + 1) * 128]
        pick = jnp.where(meta_row == 3 * k + lane_term, last, 0.0).astype(bf16)
        meta = meta + dot(pick, spread[k])
    msg_ref[BODY:SIDE, :] = meta.astype(bf16)
    msg_ref[SIDE:KEEP, :] = level_gains(part, gains)
    msg_ref[KEEP:, :] = c_half


def level_gains(part, gains):
    shape = (256, 128)
    head, level = row_mod(240, HEADS, shape)
    level = jnp.where(iota(shape, 0) >= 240, 99, level)
    own = head - part * PART_HEADS
    ok = jnp.logical_and(jnp.logical_and(own >= 0, own < PART_HEADS), level < LEVELS)
    target = jnp.where(ok, level * PART_HEADS + own, 999)
    lane = iota(shape, 1)
    packed = dot(gains[:64, :], ones_where(lane == target))
    return (packed + dot(gains[64:, :], ones_where(lane == target + 64))).astype(bf16)


def column_copies(masks, x_ref, x_buf, sems):
    copies = []
    for i, mask in enumerate(masks):
        cols = pl.ds(pl.multiple_of((spots()[2] ^ mask) * PART, 128), PART)
        copies.append(pltpu.make_async_copy(x_ref.at[:, cols], x_buf.at[i], sems.at[i]))
    return copies


def first_kernel(
    x_ref, b_ref, c_ref, decay_ref, step_ref, weight_ref,
    far_ref, cross_ref, beside_ref, within_ref, carry_ref, last_ref, bt_ref, gains_ref,
    x_buf, b_buf, c_buf, decay_buf, step_buf, weight_buf, sems,
):
    half = pl.ds(pl.multiple_of(spots()[3] * 64, 64), 64)
    copies = column_copies(FIRST, x_ref, x_buf, sems) + [
        pltpu.make_async_copy(decay_ref, decay_buf, sems.at[3]),
        pltpu.make_async_copy(step_ref, step_buf, sems.at[4]),
        pltpu.make_async_copy(b_ref, b_buf, sems.at[5]),
        pltpu.make_async_copy(weight_ref, weight_buf, sems.at[6]),
        pltpu.make_async_copy(c_ref.at[half, :], c_buf, sems.at[7]),
    ]
    for c in copies[3:] + copies[:3]:
        c.start()
    upper = ones_where(iota((128, 128), 0) <= iota((128, 128), 1))
    copies[3].wait()
    within = sum(dot(p, upper) for p in three(decay_buf[...]))
    within_ref[...] = within
    total = within[:, 127:128]
    copies[4].wait()
    carry = jnp.exp(total - within) * step_buf[...]
    pad = jnp.zeros((8, 128), f32)

    def stacked(v):
        return jnp.concatenate([p.astype(f32) for p in three(v)] + [pad], axis=0).T

    carry_t = stacked(carry).astype(bf16)
    last = stacked(within)[127:128, :]
    copies[5].wait()
    b_t = b_buf[...].astype(f32).T.astype(bf16)
    copies[6].wait()
    grown = jnp.exp(within)
    rows = [weight_buf[level] * grown for level in range(1, LEVELS + 1)]
    gains = jnp.concatenate(rows + [jnp.zeros((16, 128), f32)], axis=0).T.astype(bf16)
    carry_ref[...] = carry_t
    last_ref[...] = jnp.broadcast_to(last, (8, 128))
    bt_ref[...] = b_t
    gains_ref[...] = gains
    copies[7].wait()
    for c in copies[:3]:
        c.wait()
    for i, (mask, msg_ref) in enumerate(zip(FIRST, (far_ref, cross_ref, beside_ref))):
        part = spots()[2] ^ mask
        worker_message(part, x_buf[i], carry_t, last, b_t, gains, c_buf[...], msg_ref)


def second_kernel(
    x_ref, c_ref, carry_ref, last_ref, bt_ref, gains_ref, own_ref,
    x_buf, c_buf, sems,
):
    half = pl.ds(pl.multiple_of(spots()[3] * 64, 64), 64)
    copies = column_copies(SECOND, x_ref, x_buf, sems)
    copies.append(pltpu.make_async_copy(c_ref.at[half, :], c_buf, sems.at[1]))
    for c in copies:
        c.start()
    for c in copies:
        c.wait()
    for i, (mask, msg_ref) in enumerate(zip(SECOND, (own_ref,))):
        part = spots()[2] ^ mask
        worker_message(
            part, x_buf[i], carry_ref[...], last_ref[0:1, :], bt_ref[...], gains_ref[...], c_buf[...], msg_ref
        )


def local_kernel(
    x_hbm, b_hbm, c_hbm, step_hbm, weight_hbm, within_ref, out_ref,
    x_ref, b_ref, c_ref, step_ref, weight_ref, sems,
):
    pairs = ((x_hbm, x_ref), (b_hbm, b_ref), (c_hbm, c_ref), (step_hbm, step_ref), (weight_hbm.at[0], weight_ref))
    copies = [pltpu.make_async_copy(*p, sems.at[i]) for i, p in enumerate(pairs)]
    for c in copies:
        c.start()
    for c in copies:
        c.wait()
    scores = lax.dot_general(
        c_ref[...], b_ref[...], (((1,), (1,)), ((), ())), preferred_element_type=f32
    )
    scores = jnp.where(iota((128, 128), 0) >= iota((128, 128), 1), scores, 0.0)
    pad = jnp.zeros((128 - HEADS, 128), f32)
    within = within_ref[...]
    within_t = jnp.concatenate([within, pad], axis=0).T
    weight_t = jnp.concatenate([weight_ref[...], pad], axis=0).T
    step = step_ref[...]
    left = iota((128, 128), 1) < HEADDIM
    zero = jnp.zeros((128, 128), bf16)

    def mixing(h):
        gap = jnp.minimum(within_t[:, h : h + 1] - within[h : h + 1, :], 0.0)
        gain = weight_t[:, h : h + 1] * jnp.exp(gap)
        return (gain * scores * step[h : h + 1, :]).astype(bf16)

    for pair in range(HEADS // 2):
        cols = slice(pair * 128, (pair + 1) * 128)
        x = x_ref[:, cols]
        both = jnp.concatenate([mixing(2 * pair), mixing(2 * pair + 1)], axis=1)
        sides = jnp.concatenate([jnp.where(left, x, zero), jnp.where(left, zero, x)], axis=0)
        out_ref[:, cols] = dot(both, sides)


def total_of(meta, tile):
    return meta[3 * tile : 3 * tile + 1] + meta[3 * tile + 1 : 3 * tile + 2] + meta[3 * tile + 2 : 3 * tile + 3]


def put_total(meta, tile, total):
    row = iota((META, 128), 0)
    for k, p in enumerate(three(total)):
        meta = jnp.where(row == 3 * tile + k, p.astype(f32), meta)
    return meta


def tile_rows(tile):
    return slice(tile * STATE, (tile + 1) * STATE)


def group_kernel(*refs):
    got, (first_ref, second_ref, parts_ref, half_ref) = refs[:PLACES], refs[PLACES:]
    for mask, ref in zip(MASKS, got):
        parts_ref[spots()[2] ^ mask] = ref[:KEEP, :]
        half_ref[spots()[2] ^ mask] = ref[KEEP:, :]
    metas = [parts_ref[j, BODY:SIDE, :].astype(f32) for j in range(PLACES)]
    for tiles, out_ref in ((range(AHEAD), first_ref), (range(AHEAD, TILES), second_ref)):
        meta = jnp.zeros((META, 128), f32)
        for tile in tiles:
            rows = tile_rows(tile)
            t = [total_of(m, tile) for m in metas]
            acc = parts_ref[0, rows, :].astype(f32)
            for j in range(1, PLACES):
                acc = jnp.exp(t[j]) * acc + parts_ref[j, rows, :].astype(f32)
            out_ref[tile_rows(tile - tiles[0]), :] = acc.astype(bf16)
            meta = put_total(meta, tile - tiles[0], t[0] + t[1] + t[2] + t[3])
        out_ref[len(tiles) * STATE :, :] = meta.astype(bf16)


def flag(cond):
    return jnp.where(cond, 1.0, 0.0).astype(f32)


def joined(later, own, own_t, other, other_t):
    return jnp.exp(other_t * (1.0 - later)) * own + jnp.exp(own_t * later) * other


def pair_kernel(own_ref, other_ref, out_ref):
    later = flag(spots()[0] % 2 == 1)
    end = AHEAD * STATE
    own_meta, other_meta = own_ref[end:, :].astype(f32), other_ref[end:, :].astype(f32)
    meta = jnp.zeros((META, 128), f32)
    for tile in range(AHEAD):
        rows = tile_rows(tile)
        own_t, other_t = total_of(own_meta, tile), total_of(other_meta, tile)
        own, other = own_ref[rows, :].astype(f32), other_ref[rows, :].astype(f32)
        out_ref[rows, :] = joined(later, own, own_t, other, other_t).astype(bf16)
        meta = put_total(meta, tile, own_t + other_t)
    out_ref[end:, :] = meta.astype(bf16)


def both_kernel(own_ref, opposite_ref, out_ref):
    out_ref[0] = own_ref[...]
    out_ref[1] = opposite_ref[...]


def row_kernel(
    next_ref, pair_ref, far_ref, own_ref, opposite_ref, beside_ref, next_out, far_out, total_out
):
    odd, upper = flag(spots()[0] % 2 == 1), flag(spots()[0] >= 2)
    next_sum = jnp.zeros((META, 128), f32)
    far_sum, total_sum = next_sum, next_sum
    end, late = AHEAD * STATE, (TILES - AHEAD) * STATE
    next_meta, pair_meta, far_meta = (r[end:, :].astype(f32) for r in (next_ref, pair_ref, far_ref))
    own_meta, opposite_meta = own_ref[late:, :].astype(f32), opposite_ref[late:, :].astype(f32)
    beside_meta, last_meta = beside_ref[0, late:, :].astype(f32), beside_ref[1, late:, :].astype(f32)
    for tile in range(TILES):
        rows = tile_rows(tile)
        if tile < AHEAD:
            next_t, pair_t, far_t = (total_of(m, tile) for m in (next_meta, pair_meta, far_meta))
            next_out[rows, :] = next_ref[rows, :]
            far_out[rows, :] = far_ref[rows, :]
            pair, far = pair_ref[rows, :].astype(f32), far_ref[rows, :].astype(f32)
        else:
            spot = tile_rows(tile - AHEAD)
            own_t, next_t, opposite_t, last_t = (
                total_of(m, tile - AHEAD) for m in (own_meta, beside_meta, opposite_meta, last_meta)
            )
            own, opposite = own_ref[spot, :].astype(f32), opposite_ref[spot, :].astype(f32)
            beside, last = beside_ref[0, spot, :].astype(f32), beside_ref[1, spot, :].astype(f32)
            pair = joined(odd, own, own_t, beside, next_t)
            far = joined(1.0 - odd, opposite, opposite_t, last, last_t)
            pair_t, far_t = own_t + next_t, opposite_t + last_t
            next_out[rows, :] = beside_ref[0, spot, :]
            far_out[rows, :] = far.astype(bf16)
        total_out[rows, :] = joined(upper, pair, pair_t, far, far_t).astype(bf16)
        next_sum = put_total(next_sum, tile, next_t)
        far_sum = put_total(far_sum, tile, far_t)
        total_sum = put_total(total_sum, tile, pair_t + far_t)
    for out, meta in ((next_out, next_sum), (far_out, far_sum), (total_out, total_sum)):
        out[BODY:, :] = meta.astype(bf16)


def split(v):
    hi = v.astype(bf16)
    return jnp.concatenate([hi, (v - hi.astype(f32)).astype(bf16)], axis=0)


def wide(pieces):
    return pieces[0] if len(pieces) == 1 else jnp.concatenate(pieces, axis=1)


def gain_spread(tiles, level):
    slot = iota((128, 128), 0)
    side = jnp.where(iota((128, 128), 1) >= HEADDIM, 1, 0)
    return [
        wide([ones_where(slot == base + level * PART_HEADS + 2 * tile + side) for tile in tiles])
        for base in (0, 64)
    ]


def spread_gain(gains, spread):
    return jnp.concatenate([dot(gains, s) for s in spread], axis=0)


def block_lead(metas, place, tiles):
    return wide(
        [
            jnp.exp(sum(flag(place > j) * total_of(metas[j], tile) for j in range(PLACES - 1)))
            for tile in tiles
        ]
    )


def near_kernel(
    parts_ref, half_ref, other_ref, next_ref, pair_ref, out_ref, c_ref
):
    group = spots()[0]
    for place in range(PLACES):
        for core, ref in ((spots()[3], half_ref), (1 - spots()[3], other_ref)):
            c_ref[place, pl.ds(pl.multiple_of(core * 64, 64), 64), :] = ref[place]
    part_metas = [parts_ref[j, BODY:SIDE, :].astype(f32) for j in range(PLACES)]
    next_meta = next_ref[BODY:, :].astype(f32)
    odd, upper, third = flag(group % 2 == 1), flag(group >= 2), flag(group == 3)
    for start in range(0, TILES, 2):
        tiles = range(start, min(start + 2, TILES))
        low_b, mid_b, high_b, b3, b4, skip = [], [], [], [], [], []
        for tile in tiles:
            rows = tile_rows(tile)
            t = [total_of(m, tile) for m in part_metas]
            s0, s1 = parts_ref[0, rows, :], parts_ref[1, rows, :]
            low_b.append(s0)
            mid_b.append(split(jnp.exp(t[1]) * s0.astype(f32) + s1.astype(f32)))
            high_b.append(parts_ref[2, rows, :])
            skip.append(jnp.exp(t[2]))
            b3.append(split(odd * next_ref[rows, :].astype(f32)))
            w4 = upper * jnp.exp(third * total_of(next_meta, tile))
            b4.append(split(w4 * pair_ref[rows, :].astype(f32)))
        spread = [gain_spread(tiles, level) for level in range(4)]
        low_w, mid_w, high_w = wide(low_b), wide(mid_b), wide(high_b)
        b3_w, b4_w = wide(b3), wide(b4)
        lanes = slice(start * 128, (start + len(tiles)) * 128)
        for place in range(PLACES):
            c = c_ref[place]
            cc = jnp.concatenate([c, c], axis=1)
            gains = parts_ref[place, SIDE:, :]
            acc = spread_gain(gains, spread[2]) * dot(cc, b3_w)
            acc = acc + spread_gain(gains, spread[3]) * dot(cc, b4_w)
            if place:
                acc = acc * block_lead(part_metas, place, tiles)
            if place == 1:
                acc = acc + spread_gain(gains, spread[0]) * dot(c, low_w)
            if place == 3:
                acc = acc + spread_gain(gains, spread[0]) * dot(c, high_w)
            if place >= 2:
                term = spread_gain(gains, spread[1]) * dot(cc, mid_w)
                acc = acc + (term * wide(skip) if place == 3 else term)
            out_ref[place, :, lanes] = acc


def far_kernel(
    masks, parts_ref, c_ref, next_ref, pair_ref, r1_ref, r2_ref, r3_ref, near_ref, *out_refs
):
    group, row = spots()[:2]
    part_metas = [parts_ref[j, BODY:SIDE, :].astype(f32) for j in range(PLACES)]
    metas = [r[BODY:, :].astype(f32) for r in (next_ref, pair_ref)]
    odd_group, upper_group = flag(group % 2 == 1), flag(group >= 2)
    row_metas = [r[BODY:, :].astype(f32) for r in (r1_ref, r2_ref)]
    odd, upper = flag(row % 2 == 1), flag(row >= 2)
    second, third = flag(row == 2), flag(row == 3)
    for start in range(0, TILES, 2):
        tiles = range(start, min(start + 2, TILES))
        b5, b6 = [], []
        for tile in tiles:
            rows = tile_rows(tile)
            t = [total_of(m, tile) for m in metas]
            t1, t2 = (total_of(m, tile) for m in row_metas)
            lead = jnp.exp(odd_group * t[0] + upper_group * t[1])
            v1, v2, v3 = (r[rows, :].astype(f32) for r in (r1_ref, r2_ref, r3_ref))
            b5.append(split((lead * odd) * v1))
            w2, w3 = lead * upper * jnp.exp(t1), lead * third * jnp.exp(t1 + t2)
            b6.append(split((lead * second) * v1 + w2 * v2 + w3 * v3))
        spread = [gain_spread(tiles, level) for level in (4, 5)]
        b5_w, b6_w = wide(b5), wide(b6)
        lanes = slice(start * 128, (start + len(tiles)) * 128)
        for mask, out_ref in zip(masks, out_refs):
            place = spots()[2] ^ mask
            c = c_ref[place]
            cc = jnp.concatenate([c, c], axis=1)
            gains = parts_ref[place, SIDE:, :]
            acc = spread_gain(gains, spread[0]) * dot(cc, b5_w)
            acc = acc + spread_gain(gains, spread[1]) * dot(cc, b6_w)
            acc = acc * block_lead(part_metas, place, tiles) + near_ref[place, :, lanes]
            out_ref[:, lanes] = acc.astype(bf16)


def gate_kernel(local_ref, gate_ref, *refs):
    reached, (gated_ref, square_ref) = refs[:PLACES], refs[PLACES:]
    acc = jnp.zeros((128, 128), f32)
    for mask, reached_ref in zip(MASKS, reached):
        start = (spots()[2] ^ mask) * PART
        for tile in range(TILES):
            cols = pl.ds(pl.multiple_of(start + tile * 128, 128), 128)
            mixed = local_ref[:, cols] + reached_ref[:, tile * 128 : (tile + 1) * 128].astype(f32)
            gate = gate_ref[:, cols].astype(f32)
            gated = (mixed * (gate / (1.0 + jnp.exp(-gate)))).astype(bf16)
            gated_ref[:, cols] = gated
            full = gated.astype(f32)
            acc = acc + full * full
    square_ref[...] = acc


def norm_kernel(gated_ref, own_ref, other_ref, weight_ref, out_ref):
    mean = jnp.sum(own_ref[...] + other_ref[...], axis=1, keepdims=True) / (2.0 * COLS)
    inverse = jnp.broadcast_to(lax.rsqrt(mean + 1e-05), (128, 128))
    for pair in range(HEADS // 2):
        cols = slice(pair * 128, (pair + 1) * 128)
        out_ref[:, cols] = (
            gated_ref[:, cols].astype(f32) * inverse * weight_ref[:, cols]
        ).astype(bf16)


def call(kernel, name, outs, *args, far=0, scratch=(), flops=10**8, size=4 * 10**6, vmem=VMEM):
    whole = pl.BlockSpec(memory_space=pltpu.VMEM)
    specs = [pl.BlockSpec(memory_space=pltpu.HBM)] * far + [whole] * (len(args) - far)
    return pl.pallas_call(
        kernel,
        name=name,
        in_specs=specs,
        out_specs=[whole] * len(outs),
        out_shape=[jax.ShapeDtypeStruct(*o) for o in outs],
        scratch_shapes=list(scratch),
        cost_estimate=pl.CostEstimate(flops=flops, bytes_accessed=size, transcendentals=0),
        compiler_params=pltpu.CompilerParams(vmem_limit_bytes=vmem),
    )(*args)


def spot_of(index):
    return index // 16, index // 4 % 4, index % 4


def index_of(row, group, place):
    return row * 16 + group * 4 + place


def to_group(value, partner):
    pairs = []
    for index in range(ROWS * GROUPS * PLACES):
        row, group, place = spot_of(index)
        pairs.append((index, index_of(row, partner(group), place)))
    return lax.ppermute(value, "ctx", pairs)


def to_row(value, shift):
    pairs = []
    for index in range(ROWS * GROUPS * PLACES):
        row, group, place = spot_of(index)
        if row + shift < ROWS:
            pairs.append((index, index_of(row + shift, group, place)))
    return lax.ppermute(value, "ctx", pairs)


def to_place(value, mask):
    if not mask:
        return value
    return lax.ppermute(value, "ctx", [(i, i ^ mask) for i in range(ROWS * GROUPS * PLACES)])


def on_device(
    mixer_input,
    gate_input,
    input_proj,
    output_proj,
    step_size,
    decay_log,
    level_weight,
    norm_weight,
):
    message = ((MSG, 128), bf16)
    far, cross, beside, within, carry_t, last, b_t, gains = call(
        first_kernel,
        "first_states",
        [
            message,
            message,
            message,
            ((HEADS, 128), f32),
            ((128, 128), bf16),
            ((8, 128), f32),
            ((128, 128), bf16),
            ((128, 256), bf16),
        ],
        mixer_input,
        input_proj,
        output_proj,
        decay_log,
        step_size,
        level_weight,
        far=6,
        vmem=60 * 2**20,
        scratch=[
            pltpu.VMEM((len(FIRST), 128, PART), bf16),
            pltpu.VMEM((128, 128), bf16),
            pltpu.VMEM((64, 128), bf16),
            pltpu.VMEM((HEADS, 128), f32),
            pltpu.VMEM((HEADS, 128), f32),
            pltpu.VMEM((LEVELS + 1, HEADS, 128), f32),
            pltpu.SemaphoreType.DMA((8,)),
        ],
    )
    (own,) = call(
        second_kernel,
        "second_states",
        [message],
        mixer_input,
        output_proj,
        carry_t,
        last,
        b_t,
        gains,
        far=2,
        flops=4 * 10**10,
        scratch=[
            pltpu.VMEM((len(SECOND), 128, PART), bf16),
            pltpu.VMEM((64, 128), bf16),
            pltpu.SemaphoreType.DMA((2,)),
        ],
    )
    (local,) = call(
        local_kernel,
        "local_part",
        [((128, COLS), f32)],
        mixer_input,
        input_proj,
        output_proj,
        step_size,
        level_weight,
        within,
        far=5,
        scratch=[
            pltpu.VMEM((128, COLS), bf16),
            pltpu.VMEM((128, 128), bf16),
            pltpu.VMEM((128, 128), bf16),
            pltpu.VMEM((HEADS, 128), f32),
            pltpu.VMEM((HEADS, 128), f32),
            pltpu.SemaphoreType.DMA((5,)),
        ],
        flops=10**10,
        size=10**7,
    )
    got = [to_place(v, mask) for mask, v in zip(MASKS, (far, cross, beside, own))]
    ahead = ((AHEAD * STATE + META, 128), bf16)
    behind = (((TILES - AHEAD) * STATE + META, 128), bf16)
    whole = ((BODY + META, 128), bf16)
    sums, late_sums, parts, halves = call(
        group_kernel,
        "group_state",
        [ahead, behind, ((PLACES, KEEP, 128), bf16), ((PLACES, 64, 128), bf16)],
        *got,
    )
    beside = to_group(sums, lambda g: g ^ 1)
    opposite = to_group(late_sums, lambda g: 3 - g)
    (pair,) = call(pair_kernel, "pair_state", [ahead], sums, beside)
    (both,) = call(
        both_kernel, "two_states", [((2,) + behind[0], bf16)], late_sums, opposite
    )
    late_beside = to_group(both, lambda g: g ^ 1)
    other_pair = to_group(pair, lambda g: 3 - g)
    halves_now, _ = lax.optimization_barrier((halves, pair))
    others = lax.ppermute(halves_now, "head", [(0, 1), (1, 0)])
    neighbour, other_pair, total = call(
        row_kernel,
        "row_state",
        [whole, whole, whole],
        beside,
        pair,
        other_pair,
        late_sums,
        opposite,
        late_beside,
    )
    rows = [to_row(total, k) for k in (1, 2, 3)]
    near, c_all = call(
        near_kernel,
        "near_levels",
        [((PLACES, 128, PART), f32), ((PLACES, 128, 128), bf16)],
        parts,
        halves,
        others,
        neighbour,
        other_pair,
        flops=10**10,
    )
    reached = []
    for masks in (FIRST, SECOND):
        reached += call(
            functools.partial(far_kernel, masks),
            "far_levels",
            [((128, PART), bf16)] * len(masks),
                parts,
            c_all,
            neighbour,
            other_pair,
            *rows,
            near,
                flops=10**10,
        )
    back = [to_place(v, mask) for mask, v in zip(MASKS, reached)]
    gated, square = call(
        gate_kernel,
        "gate",
        [((128, COLS), bf16), ((128, 128), f32)],
        local,
        gate_input,
        *back,
    )
    other = lax.ppermute(square, "head", [(0, 1), (1, 0)])
    (out,) = call(
        norm_kernel,
        "norm",
        [((128, COLS), bf16)],
        gated,
        square,
        other,
        norm_weight.reshape(1, COLS),
    )
    return out


def solution(mesh):
    in_specs = (
        P(("seq", "ctx"), "head"),
        P(("seq", "ctx"), "head"),
        P(("seq", "ctx"), None),
        P(("seq", "ctx"), None),
        P("head", ("seq", "ctx")),
        P("head", ("seq", "ctx")),
        P(None, "head", ("seq", "ctx")),
        P("head"),
    )
    out_specs = P(("seq", "ctx"), "head")
    return jax.shard_map(
        on_device, mesh=mesh, in_specs=in_specs, out_specs=out_specs, check_vma=False
    )
```

```python
import functools

import jax
import jax.numpy as jnp
from jax import lax
from jax.experimental import pallas as pl
from jax.experimental.pallas import tpu as pltpu
from jax.sharding import PartitionSpec as P

ROWS, GROUPS, PLACES = 4, 4, 4
BLOCK = 128
STATE = 128
HEADDIM = 64
HEADS = 40
COLS = HEADS * HEADDIM
PART_HEADS = HEADS // PLACES
PART = COLS // PLACES
TILES = PART // 128
BODY = TILES * STATE
AHEAD = 3
META = 16
SIDE = BODY + META
KEEP = SIDE + 64
MSG = KEEP + 64
LEVELS = 6
FIRST, SECOND = (2, 3, 1), (0,)
MASKS = FIRST + SECOND
f32, bf16, i32 = jnp.float32, jnp.bfloat16, jnp.int32
VMEM = 24 * 2**20


def spots():
    position = lax.axis_index("ctx")
    return position // 4 % 4, position // 16, position % 4, lax.axis_index("head")


def dot(a, b):
    return jnp.dot(a, b, preferred_element_type=f32)


def three(v):
    hi = v.astype(bf16)
    rest = v - hi.astype(f32)
    mid = rest.astype(bf16)
    return hi, mid, (rest - mid.astype(f32)).astype(bf16)


def iota(shape, dim):
    return lax.broadcasted_iota(i32, shape, dim)


def ones_where(cond):
    return jnp.where(cond, 1.0, 0.0).astype(bf16)


def row_mod(rows, period, shape):
    r = iota(shape, 0)
    turn = jnp.zeros(shape, i32)
    for k in range(period, rows, period):
        turn = turn + jnp.where(r >= k, 1, 0)
    return r - turn * period, turn


def worker_message(part, x, carry_t, last, b_t, gains, c_half, msg_ref):
    head, _ = row_mod(120, HEADS, (128, 128))
    head = jnp.where(iota((128, 128), 0) >= 120, 999, head)
    side = jnp.where(iota((128, 128), 1) >= HEADDIM, 1, 0)
    lane = iota((META, 128), 1)
    lane_term = jnp.where(lane >= 2 * HEADS, 2, jnp.where(lane >= HEADS, 1, 0))
    meta_row = iota((META, 128), 0)
    base = part * PART_HEADS
    spread = [ones_where(head - base == 2 * k + side) for k in range(TILES)]
    scaled = (dot(carry_t, jnp.concatenate(spread, axis=1)) * x.astype(f32)).astype(bf16)
    state = dot(b_t, scaled).astype(bf16)
    meta = jnp.zeros((META, 128), f32)
    for k in range(TILES):
        msg_ref[k * STATE : (k + 1) * STATE, :] = state[:, k * 128 : (k + 1) * 128]
        pick = jnp.where(meta_row == 3 * k + lane_term, last, 0.0).astype(bf16)
        meta = meta + dot(pick, spread[k])
    msg_ref[BODY:SIDE, :] = meta.astype(bf16)
    msg_ref[SIDE:KEEP, :] = level_gains(part, gains)
    msg_ref[KEEP:, :] = c_half


def level_gains(part, gains):
    shape = (256, 128)
    head, level = row_mod(240, HEADS, shape)
    level = jnp.where(iota(shape, 0) >= 240, 99, level)
    own = head - part * PART_HEADS
    ok = jnp.logical_and(jnp.logical_and(own >= 0, own < PART_HEADS), level < LEVELS)
    target = jnp.where(ok, level * PART_HEADS + own, 999)
    lane = iota(shape, 1)
    packed = dot(gains[:64, :], ones_where(lane == target))
    return (packed + dot(gains[64:, :], ones_where(lane == target + 64))).astype(bf16)


def column_copies(masks, x_ref, x_buf, sems):
    copies = []
    for i, mask in enumerate(masks):
        cols = pl.ds(pl.multiple_of((spots()[2] ^ mask) * PART, 128), PART)
        copies.append(pltpu.make_async_copy(x_ref.at[:, cols], x_buf.at[i], sems.at[i]))
    return copies


def first_kernel(
    x_ref, b_ref, c_ref, decay_ref, step_ref, weight_ref,
    far_ref, cross_ref, beside_ref, within_ref, carry_ref, last_ref, bt_ref, gains_ref,
    x_buf, b_buf, c_buf, decay_buf, step_buf, weight_buf, sems,
):
    half = pl.ds(pl.multiple_of(spots()[3] * 64, 64), 64)
    copies = column_copies(FIRST, x_ref, x_buf, sems) + [
        pltpu.make_async_copy(decay_ref, decay_buf, sems.at[3]),
        pltpu.make_async_copy(step_ref, step_buf, sems.at[4]),
        pltpu.make_async_copy(b_ref, b_buf, sems.at[5]),
        pltpu.make_async_copy(weight_ref, weight_buf, sems.at[6]),
        pltpu.make_async_copy(c_ref.at[half, :], c_buf, sems.at[7]),
    ]
    for c in copies[3:] + copies[:3]:
        c.start()
    upper = ones_where(iota((128, 128), 0) <= iota((128, 128), 1))
    copies[3].wait()
    within = sum(dot(p, upper) for p in three(decay_buf[...]))
    within_ref[...] = within
    total = within[:, 127:128]
    copies[4].wait()
    carry = jnp.exp(total - within) * step_buf[...]
    pad = jnp.zeros((8, 128), f32)

    def stacked(v):
        return jnp.concatenate([p.astype(f32) for p in three(v)] + [pad], axis=0).T

    carry_t = stacked(carry).astype(bf16)
    last = stacked(within)[127:128, :]
    copies[5].wait()
    b_t = b_buf[...].astype(f32).T.astype(bf16)
    copies[6].wait()
    grown = jnp.exp(within)
    rows = [weight_buf[level] * grown for level in range(1, LEVELS + 1)]
    gains = jnp.concatenate(rows + [jnp.zeros((16, 128), f32)], axis=0).T.astype(bf16)
    carry_ref[...] = carry_t
    last_ref[...] = jnp.broadcast_to(last, (8, 128))
    bt_ref[...] = b_t
    gains_ref[...] = gains
    copies[7].wait()
    for c in copies[:3]:
        c.wait()
    for i, (mask, msg_ref) in enumerate(zip(FIRST, (far_ref, cross_ref, beside_ref))):
        part = spots()[2] ^ mask
        worker_message(part, x_buf[i], carry_t, last, b_t, gains, c_buf[...], msg_ref)


def second_kernel(
    x_ref, c_ref, carry_ref, last_ref, bt_ref, gains_ref, own_ref,
    x_buf, c_buf, sems,
):
    half = pl.ds(pl.multiple_of(spots()[3] * 64, 64), 64)
    copies = column_copies(SECOND, x_ref, x_buf, sems)
    copies.append(pltpu.make_async_copy(c_ref.at[half, :], c_buf, sems.at[1]))
    for c in copies:
        c.start()
    for c in copies:
        c.wait()
    for i, (mask, msg_ref) in enumerate(zip(SECOND, (own_ref,))):
        part = spots()[2] ^ mask
        worker_message(
            part, x_buf[i], carry_ref[...], last_ref[0:1, :], bt_ref[...], gains_ref[...], c_buf[...], msg_ref
        )


def local_kernel(
    x_hbm, b_hbm, c_hbm, step_hbm, weight_hbm, gate_hbm, within_ref, out_ref, silu_ref,
    x_ref, b_ref, c_ref, step_ref, weight_ref, gate_ref, sems,
):
    pairs = (
        (x_hbm, x_ref), (b_hbm, b_ref), (c_hbm, c_ref), (step_hbm, step_ref),
        (weight_hbm.at[0], weight_ref), (gate_hbm, gate_ref),
    )
    copies = [pltpu.make_async_copy(*p, sems.at[i]) for i, p in enumerate(pairs)]
    for c in copies:
        c.start()
    for c in copies:
        c.wait()
    scores = lax.dot_general(
        c_ref[...], b_ref[...], (((1,), (1,)), ((), ())), preferred_element_type=f32
    )
    scores = jnp.where(iota((128, 128), 0) >= iota((128, 128), 1), scores, 0.0)
    pad = jnp.zeros((128 - HEADS, 128), f32)
    within = within_ref[...]
    within_t = jnp.concatenate([within, pad], axis=0).T
    weight_t = jnp.concatenate([weight_ref[...], pad], axis=0).T
    step = step_ref[...]
    left = iota((128, 128), 1) < HEADDIM
    zero = jnp.zeros((128, 128), bf16)

    def mixing(h):
        gap = jnp.minimum(within_t[:, h : h + 1] - within[h : h + 1, :], 0.0)
        gain = weight_t[:, h : h + 1] * jnp.exp(gap)
        return (gain * scores * step[h : h + 1, :]).astype(bf16)

    for pair in range(HEADS // 2):
        cols = slice(pair * 128, (pair + 1) * 128)
        x = x_ref[:, cols]
        both = jnp.concatenate([mixing(2 * pair), mixing(2 * pair + 1)], axis=1)
        sides = jnp.concatenate([jnp.where(left, x, zero), jnp.where(left, zero, x)], axis=0)
        out_ref[:, cols] = dot(both, sides)
        gate = gate_ref[:, cols].astype(f32)
        silu_ref[:, cols] = gate / (1.0 + jnp.exp(-gate))


def total_of(meta, tile):
    return meta[3 * tile : 3 * tile + 1] + meta[3 * tile + 1 : 3 * tile + 2] + meta[3 * tile + 2 : 3 * tile + 3]


def put_total(meta, tile, total):
    row = iota((META, 128), 0)
    for k, p in enumerate(three(total)):
        meta = jnp.where(row == 3 * tile + k, p.astype(f32), meta)
    return meta


def tile_rows(tile):
    return slice(tile * STATE, (tile + 1) * STATE)


def group_kernel(*refs):
    got, (first_ref, second_ref, parts_ref, half_ref) = refs[:PLACES], refs[PLACES:]
    for mask, ref in zip(MASKS, got):
        parts_ref[spots()[2] ^ mask] = ref[:KEEP, :]
        half_ref[spots()[2] ^ mask] = ref[KEEP:, :]
    metas = [parts_ref[j, BODY:SIDE, :].astype(f32) for j in range(PLACES)]
    for tiles, out_ref in ((range(AHEAD), first_ref), (range(AHEAD, TILES), second_ref)):
        meta = jnp.zeros((META, 128), f32)
        for tile in tiles:
            rows = tile_rows(tile)
            t = [total_of(m, tile) for m in metas]
            acc = parts_ref[0, rows, :].astype(f32)
            for j in range(1, PLACES):
                acc = jnp.exp(t[j]) * acc + parts_ref[j, rows, :].astype(f32)
            out_ref[tile_rows(tile - tiles[0]), :] = acc.astype(bf16)
            meta = put_total(meta, tile - tiles[0], t[0] + t[1] + t[2] + t[3])
        out_ref[len(tiles) * STATE :, :] = meta.astype(bf16)


def flag(cond):
    return jnp.where(cond, 1.0, 0.0).astype(f32)


def joined(later, own, own_t, other, other_t):
    return jnp.exp(other_t * (1.0 - later)) * own + jnp.exp(own_t * later) * other


def pair_kernel(own_ref, other_ref, out_ref):
    later = flag(spots()[0] % 2 == 1)
    end = AHEAD * STATE
    own_meta, other_meta = own_ref[end:, :].astype(f32), other_ref[end:, :].astype(f32)
    meta = jnp.zeros((META, 128), f32)
    for tile in range(AHEAD):
        rows = tile_rows(tile)
        own_t, other_t = total_of(own_meta, tile), total_of(other_meta, tile)
        own, other = own_ref[rows, :].astype(f32), other_ref[rows, :].astype(f32)
        out_ref[rows, :] = joined(later, own, own_t, other, other_t).astype(bf16)
        meta = put_total(meta, tile, own_t + other_t)
    out_ref[end:, :] = meta.astype(bf16)


def both_kernel(own_ref, opposite_ref, out_ref):
    out_ref[0] = own_ref[...]
    out_ref[1] = opposite_ref[...]


def row_kernel(
    next_ref, pair_ref, far_ref, own_ref, opposite_ref, beside_ref, next_out, far_out, total_out
):
    odd, upper = flag(spots()[0] % 2 == 1), flag(spots()[0] >= 2)
    next_sum = jnp.zeros((META, 128), f32)
    far_sum, total_sum = next_sum, next_sum
    end, late = AHEAD * STATE, (TILES - AHEAD) * STATE
    next_meta, pair_meta, far_meta = (r[end:, :].astype(f32) for r in (next_ref, pair_ref, far_ref))
    own_meta, opposite_meta = own_ref[late:, :].astype(f32), opposite_ref[late:, :].astype(f32)
    beside_meta, last_meta = beside_ref[0, late:, :].astype(f32), beside_ref[1, late:, :].astype(f32)
    for tile in range(TILES):
        rows = tile_rows(tile)
        if tile < AHEAD:
            next_t, pair_t, far_t = (total_of(m, tile) for m in (next_meta, pair_meta, far_meta))
            next_out[rows, :] = next_ref[rows, :]
            far_out[rows, :] = far_ref[rows, :]
            pair, far = pair_ref[rows, :].astype(f32), far_ref[rows, :].astype(f32)
        else:
            spot = tile_rows(tile - AHEAD)
            own_t, next_t, opposite_t, last_t = (
                total_of(m, tile - AHEAD) for m in (own_meta, beside_meta, opposite_meta, last_meta)
            )
            own, opposite = own_ref[spot, :].astype(f32), opposite_ref[spot, :].astype(f32)
            beside, last = beside_ref[0, spot, :].astype(f32), beside_ref[1, spot, :].astype(f32)
            pair = joined(odd, own, own_t, beside, next_t)
            far = joined(1.0 - odd, opposite, opposite_t, last, last_t)
            pair_t, far_t = own_t + next_t, opposite_t + last_t
            next_out[rows, :] = beside_ref[0, spot, :]
            far_out[rows, :] = far.astype(bf16)
        total_out[rows, :] = joined(upper, pair, pair_t, far, far_t).astype(bf16)
        next_sum = put_total(next_sum, tile, next_t)
        far_sum = put_total(far_sum, tile, far_t)
        total_sum = put_total(total_sum, tile, pair_t + far_t)
    for out, meta in ((next_out, next_sum), (far_out, far_sum), (total_out, total_sum)):
        out[BODY:, :] = meta.astype(bf16)


def split(v):
    hi = v.astype(bf16)
    return jnp.concatenate([hi, (v - hi.astype(f32)).astype(bf16)], axis=0)


def wide(pieces):
    return pieces[0] if len(pieces) == 1 else jnp.concatenate(pieces, axis=1)


def gain_spread(tiles, level):
    slot = iota((128, 128), 0)
    side = jnp.where(iota((128, 128), 1) >= HEADDIM, 1, 0)
    return [
        wide([ones_where(slot == base + level * PART_HEADS + 2 * tile + side) for tile in tiles])
        for base in (0, 64)
    ]


def spread_gain(gains, spread):
    return jnp.concatenate([dot(gains, s) for s in spread], axis=0)


def block_lead(metas, place, tiles):
    return wide(
        [
            jnp.exp(sum(flag(place > j) * total_of(metas[j], tile) for j in range(PLACES - 1)))
            for tile in tiles
        ]
    )


def near_kernel(
    parts_ref, half_ref, other_ref, next_ref, pair_ref, out_ref, c_ref, gain_ref
):
    group = spots()[0]
    for place in range(PLACES):
        for core, ref in ((spots()[3], half_ref), (1 - spots()[3], other_ref)):
            c_ref[place, pl.ds(pl.multiple_of(core * 64, 64), 64), :] = ref[place]
    part_metas = [parts_ref[j, BODY:SIDE, :].astype(f32) for j in range(PLACES)]
    next_meta = next_ref[BODY:, :].astype(f32)
    odd, upper, third = flag(group % 2 == 1), flag(group >= 2), flag(group == 3)
    for start in range(0, TILES, 2):
        tiles = range(start, min(start + 2, TILES))
        low_b, mid_b, high_b, b3, b4, skip = [], [], [], [], [], []
        for tile in tiles:
            rows = tile_rows(tile)
            t = [total_of(m, tile) for m in part_metas]
            s0, s1 = parts_ref[0, rows, :], parts_ref[1, rows, :]
            low_b.append(s0)
            mid_b.append(split(jnp.exp(t[1]) * s0.astype(f32) + s1.astype(f32)))
            high_b.append(parts_ref[2, rows, :])
            skip.append(jnp.exp(t[2]))
            b3.append(split(odd * next_ref[rows, :].astype(f32)))
            w4 = upper * jnp.exp(third * total_of(next_meta, tile))
            b4.append(split(w4 * pair_ref[rows, :].astype(f32)))
        spread = [gain_spread(tiles, level) for level in range(LEVELS)]
        low_w, mid_w, high_w = wide(low_b), wide(mid_b), wide(high_b)
        b3_w, b4_w = wide(b3), wide(b4)
        lanes = slice(start * 128, (start + len(tiles)) * 128)
        for place in range(PLACES):
            c = c_ref[place]
            cc = jnp.concatenate([c, c], axis=1)
            gains = parts_ref[place, SIDE:, :]
            acc = spread_gain(gains, spread[2]) * dot(cc, b3_w)
            acc = acc + spread_gain(gains, spread[3]) * dot(cc, b4_w)
            lead = block_lead(part_metas, place, tiles)
            for k in range(2):
                gain_ref[place, k, :, lanes] = spread_gain(gains, spread[4 + k]) * lead
            acc = acc * lead
            if place == 1:
                acc = acc + spread_gain(gains, spread[0]) * dot(c, low_w)
            if place == 3:
                acc = acc + spread_gain(gains, spread[0]) * dot(c, high_w)
            if place >= 2:
                term = spread_gain(gains, spread[1]) * dot(cc, mid_w)
                acc = acc + (term * wide(skip) if place == 3 else term)
            out_ref[place, :, lanes] = acc


def far_kernel(
    masks, c_ref, gain_ref, next_ref, pair_ref, r1_ref, r2_ref, r3_ref, near_ref, *out_refs
):
    group, row = spots()[:2]
    metas = [r[BODY:, :].astype(f32) for r in (next_ref, pair_ref)]
    odd_group, upper_group = flag(group % 2 == 1), flag(group >= 2)
    row_metas = [r[BODY:, :].astype(f32) for r in (r1_ref, r2_ref)]
    odd, upper = flag(row % 2 == 1), flag(row >= 2)
    second, third = flag(row == 2), flag(row == 3)
    for start in range(0, TILES, 2):
        tiles = range(start, min(start + 2, TILES))
        b5, b6 = [], []
        for tile in tiles:
            rows = tile_rows(tile)
            t = [total_of(m, tile) for m in metas]
            t1, t2 = (total_of(m, tile) for m in row_metas)
            lead = jnp.exp(odd_group * t[0] + upper_group * t[1])
            v1, v2, v3 = (r[rows, :].astype(f32) for r in (r1_ref, r2_ref, r3_ref))
            b5.append(split((lead * odd) * v1))
            w2, w3 = lead * upper * jnp.exp(t1), lead * third * jnp.exp(t1 + t2)
            b6.append(split((lead * second) * v1 + w2 * v2 + w3 * v3))
        b5_w, b6_w = wide(b5), wide(b6)
        lanes = slice(start * 128, (start + len(tiles)) * 128)
        for mask, out_ref in zip(masks, out_refs):
            place = spots()[2] ^ mask
            c = c_ref[place]
            cc = jnp.concatenate([c, c], axis=1)
            acc = gain_ref[place, 0, :, lanes] * dot(cc, b5_w)
            acc = acc + gain_ref[place, 1, :, lanes] * dot(cc, b6_w)
            acc = acc + near_ref[place, :, lanes]
            out_ref[:, lanes] = acc.astype(bf16)


def gate_kernel(local_ref, silu_ref, *refs):
    reached, (gated_ref, square_ref) = refs[:PLACES], refs[PLACES:]
    acc = jnp.zeros((128, 128), f32)
    for mask, reached_ref in zip(MASKS, reached):
        start = (spots()[2] ^ mask) * PART
        for tile in range(TILES):
            cols = pl.ds(pl.multiple_of(start + tile * 128, 128), 128)
            mixed = local_ref[:, cols] + reached_ref[:, tile * 128 : (tile + 1) * 128].astype(f32)
            gated = (mixed * silu_ref[:, cols]).astype(bf16)
            gated_ref[:, cols] = gated
            full = gated.astype(f32)
            acc = acc + full * full
    square_ref[...] = acc


def norm_kernel(gated_ref, own_ref, other_ref, weight_ref, out_ref):
    mean = jnp.sum(own_ref[...] + other_ref[...], axis=1, keepdims=True) / (2.0 * COLS)
    inverse = jnp.broadcast_to(lax.rsqrt(mean + 1e-05), (128, 128))
    for pair in range(HEADS // 2):
        cols = slice(pair * 128, (pair + 1) * 128)
        out_ref[:, cols] = (
            gated_ref[:, cols].astype(f32) * inverse * weight_ref[:, cols]
        ).astype(bf16)


def call(kernel, name, outs, *args, far=0, scratch=(), flops=10**8, size=4 * 10**6, vmem=VMEM):
    whole = pl.BlockSpec(memory_space=pltpu.VMEM)
    specs = [pl.BlockSpec(memory_space=pltpu.HBM)] * far + [whole] * (len(args) - far)
    return pl.pallas_call(
        kernel,
        name=name,
        in_specs=specs,
        out_specs=[whole] * len(outs),
        out_shape=[jax.ShapeDtypeStruct(*o) for o in outs],
        scratch_shapes=list(scratch),
        cost_estimate=pl.CostEstimate(flops=flops, bytes_accessed=size, transcendentals=0),
        compiler_params=pltpu.CompilerParams(vmem_limit_bytes=vmem),
    )(*args)


def spot_of(index):
    return index // 16, index // 4 % 4, index % 4


def index_of(row, group, place):
    return row * 16 + group * 4 + place


def to_group(value, partner):
    pairs = []
    for index in range(ROWS * GROUPS * PLACES):
        row, group, place = spot_of(index)
        pairs.append((index, index_of(row, partner(group), place)))
    return lax.ppermute(value, "ctx", pairs)


def to_row(value, shift):
    pairs = []
    for index in range(ROWS * GROUPS * PLACES):
        row, group, place = spot_of(index)
        if row + shift < ROWS:
            pairs.append((index, index_of(row + shift, group, place)))
    return lax.ppermute(value, "ctx", pairs)


def to_place(value, mask):
    if not mask:
        return value
    return lax.ppermute(value, "ctx", [(i, i ^ mask) for i in range(ROWS * GROUPS * PLACES)])


def on_device(
    mixer_input,
    gate_input,
    input_proj,
    output_proj,
    step_size,
    decay_log,
    level_weight,
    norm_weight,
):
    message = ((MSG, 128), bf16)
    far, cross, beside, within, carry_t, last, b_t, gains = call(
        first_kernel,
        "first_states",
        [
            message,
            message,
            message,
            ((HEADS, 128), f32),
            ((128, 128), bf16),
            ((8, 128), f32),
            ((128, 128), bf16),
            ((128, 256), bf16),
        ],
        mixer_input,
        input_proj,
        output_proj,
        decay_log,
        step_size,
        level_weight,
        far=6,
        vmem=60 * 2**20,
        scratch=[
            pltpu.VMEM((len(FIRST), 128, PART), bf16),
            pltpu.VMEM((128, 128), bf16),
            pltpu.VMEM((64, 128), bf16),
            pltpu.VMEM((HEADS, 128), f32),
            pltpu.VMEM((HEADS, 128), f32),
            pltpu.VMEM((LEVELS + 1, HEADS, 128), f32),
            pltpu.SemaphoreType.DMA((8,)),
        ],
    )
    (own,) = call(
        second_kernel,
        "second_states",
        [message],
        mixer_input,
        output_proj,
        carry_t,
        last,
        b_t,
        gains,
        far=2,
        flops=4 * 10**10,
        scratch=[
            pltpu.VMEM((len(SECOND), 128, PART), bf16),
            pltpu.VMEM((64, 128), bf16),
            pltpu.SemaphoreType.DMA((2,)),
        ],
    )
    local, silu = call(
        local_kernel,
        "local_part",
        [((128, COLS), f32), ((128, COLS), f32)],
        mixer_input,
        input_proj,
        output_proj,
        step_size,
        level_weight,
        gate_input,
        within,
        far=6,
        scratch=[
            pltpu.VMEM((128, COLS), bf16),
            pltpu.VMEM((128, 128), bf16),
            pltpu.VMEM((128, 128), bf16),
            pltpu.VMEM((HEADS, 128), f32),
            pltpu.VMEM((HEADS, 128), f32),
            pltpu.VMEM((128, COLS), bf16),
            pltpu.SemaphoreType.DMA((6,)),
        ],
        flops=10**10,
        size=10**7,
    )
    got = [to_place(v, mask) for mask, v in zip(MASKS, (far, cross, beside, own))]
    ahead = ((AHEAD * STATE + META, 128), bf16)
    behind = (((TILES - AHEAD) * STATE + META, 128), bf16)
    whole = ((BODY + META, 128), bf16)
    sums, late_sums, parts, halves = call(
        group_kernel,
        "group_state",
        [ahead, behind, ((PLACES, KEEP, 128), bf16), ((PLACES, 64, 128), bf16)],
        *got,
    )
    opposite = to_group(late_sums, lambda g: 3 - g)
    (both,) = call(
        both_kernel, "two_states", [((2,) + behind[0], bf16)], late_sums, opposite
    )
    beside = to_group(sums, lambda g: g ^ 1)
    (pair,) = call(pair_kernel, "pair_state", [ahead], sums, beside)
    late_beside = to_group(both, lambda g: g ^ 1)
    other_pair = to_group(pair, lambda g: 3 - g)
    halves_now, _ = lax.optimization_barrier((halves, pair))
    others = lax.ppermute(halves_now, "head", [(0, 1), (1, 0)])
    neighbour, other_pair, total = call(
        row_kernel,
        "row_state",
        [whole, whole, whole],
        beside,
        pair,
        other_pair,
        late_sums,
        opposite,
        late_beside,
    )
    rows = [to_row(total, k) for k in (1, 2, 3)]
    near, c_all, far_gains = call(
        near_kernel,
        "near_levels",
        [((PLACES, 128, PART), f32), ((PLACES, 128, 128), bf16), ((PLACES, 2, 128, PART), f32)],
        parts,
        halves,
        others,
        neighbour,
        other_pair,
        flops=10**10,
    )
    reached = []
    for masks in (FIRST, SECOND):
        reached += call(
            functools.partial(far_kernel, masks),
            "far_levels",
            [((128, PART), bf16)] * len(masks),
                c_all,
            far_gains,
            neighbour,
            other_pair,
            *rows,
            near,
                flops=10**10,
        )
    back = [to_place(v, mask) for mask, v in zip(MASKS, reached)]
    gated, square = call(
        gate_kernel,
        "gate",
        [((128, COLS), bf16), ((128, 128), f32)],
        local,
        silu,
        *back,
    )
    other = lax.ppermute(square, "head", [(0, 1), (1, 0)])
    (out,) = call(
        norm_kernel,
        "norm",
        [((128, COLS), bf16)],
        gated,
        square,
        other,
        norm_weight.reshape(1, COLS),
    )
    return out


def solution(mesh):
    in_specs = (
        P(("seq", "ctx"), "head"),
        P(("seq", "ctx"), "head"),
        P(("seq", "ctx"), None),
        P(("seq", "ctx"), None),
        P("head", ("seq", "ctx")),
        P("head", ("seq", "ctx")),
        P(None, "head", ("seq", "ctx")),
        P("head"),
    )
    out_specs = P(("seq", "ctx"), "head")
    return jax.shard_map(
        on_device, mesh=mesh, in_specs=in_specs, out_specs=out_specs, check_vma=False
    )
```

```python
import functools

import jax
import jax.numpy as jnp
from jax import lax
from jax.experimental import pallas as pl
from jax.experimental.pallas import tpu as pltpu
from jax.sharding import PartitionSpec as P

ROWS, GROUPS, PLACES = 4, 4, 4
BLOCK = 128
STATE = 128
HEADDIM = 64
HEADS = 40
COLS = HEADS * HEADDIM
PART_HEADS = HEADS // PLACES
PART = COLS // PLACES
TILES = PART // 128
BODY = TILES * STATE
AHEAD = 3
META = 16
MSG = BODY + META
EXTRA = 192
LEVELS = 6
FIRST, SECOND = (2, 3, 1), (0,)
MASKS = FIRST + SECOND
f32, bf16, i32 = jnp.float32, jnp.bfloat16, jnp.int32
VMEM = 24 * 2**20


def spots():
    position = lax.axis_index("ctx")
    return position // 4 % 4, position // 16, position % 4, lax.axis_index("head")


def dot(a, b):
    return jnp.dot(a, b, preferred_element_type=f32)


def three(v):
    hi = v.astype(bf16)
    rest = v - hi.astype(f32)
    mid = rest.astype(bf16)
    return hi, mid, (rest - mid.astype(f32)).astype(bf16)


def iota(shape, dim):
    return lax.broadcasted_iota(i32, shape, dim)


def ones_where(cond):
    return jnp.where(cond, 1.0, 0.0).astype(bf16)


def row_mod(rows, period, shape):
    r = iota(shape, 0)
    turn = jnp.zeros(shape, i32)
    for k in range(period, rows, period):
        turn = turn + jnp.where(r >= k, 1, 0)
    return r - turn * period, turn


def worker_message(part, x, carry_t, last, b_t, gains, c, msg_ref, side_ref):
    head, _ = row_mod(120, HEADS, (128, 128))
    head = jnp.where(iota((128, 128), 0) >= 120, 999, head)
    side = jnp.where(iota((128, 128), 1) >= HEADDIM, 1, 0)
    lane = iota((META, 128), 1)
    lane_term = jnp.where(lane >= 2 * HEADS, 2, jnp.where(lane >= HEADS, 1, 0))
    meta_row = iota((META, 128), 0)
    base = part * PART_HEADS
    spread = [ones_where(head - base == 2 * k + side) for k in range(TILES)]
    scaled = (dot(carry_t, jnp.concatenate(spread, axis=1)) * x.astype(f32)).astype(bf16)
    state = dot(b_t, scaled).astype(bf16)
    meta = jnp.zeros((META, 128), f32)
    for k in range(TILES):
        msg_ref[k * STATE : (k + 1) * STATE, :] = state[:, k * 128 : (k + 1) * 128]
        pick = jnp.where(meta_row == 3 * k + lane_term, last, 0.0).astype(bf16)
        meta = meta + dot(pick, spread[k])
    msg_ref[BODY:, :] = meta.astype(bf16)
    side_ref[:128, :] = c
    side_ref[128:, :] = level_gains(part, gains)


def level_gains(part, gains):
    shape = (256, 128)
    head, level = row_mod(240, HEADS, shape)
    level = jnp.where(iota(shape, 0) >= 240, 99, level)
    own = head - part * PART_HEADS
    ok = jnp.logical_and(jnp.logical_and(own >= 0, own < PART_HEADS), level < LEVELS)
    target = jnp.where(ok, level * PART_HEADS + own, 999)
    lane = iota(shape, 1)
    packed = dot(gains[:64, :], ones_where(lane == target))
    return (packed + dot(gains[64:, :], ones_where(lane == target + 64))).astype(bf16)


def column_copies(masks, x_ref, x_buf, sems):
    copies = []
    for i, mask in enumerate(masks):
        cols = pl.ds(pl.multiple_of((spots()[2] ^ mask) * PART, 128), PART)
        copies.append(pltpu.make_async_copy(x_ref.at[:, cols], x_buf.at[i], sems.at[i]))
    return copies


def first_kernel(
    x_ref, b_ref, c_ref, decay_ref, step_ref, weight_ref,
    far_ref, cross_ref, beside_ref, far_side, cross_side, beside_side, within_ref, carry_ref, last_ref, bt_ref, gains_ref,
    x_buf, b_buf, c_buf, decay_buf, step_buf, weight_buf, sems,
):
    copies = column_copies(FIRST, x_ref, x_buf, sems) + [
        pltpu.make_async_copy(decay_ref, decay_buf, sems.at[3]),
        pltpu.make_async_copy(step_ref, step_buf, sems.at[4]),
        pltpu.make_async_copy(b_ref, b_buf, sems.at[5]),
        pltpu.make_async_copy(weight_ref, weight_buf, sems.at[6]),
        pltpu.make_async_copy(c_ref, c_buf, sems.at[7]),
    ]
    for c in copies[3:] + copies[:3]:
        c.start()
    upper = ones_where(iota((128, 128), 0) <= iota((128, 128), 1))
    copies[3].wait()
    within = sum(dot(p, upper) for p in three(decay_buf[...]))
    within_ref[...] = within
    total = within[:, 127:128]
    copies[4].wait()
    carry = jnp.exp(total - within) * step_buf[...]
    pad = jnp.zeros((8, 128), f32)

    def stacked(v):
        return jnp.concatenate([p.astype(f32) for p in three(v)] + [pad], axis=0).T

    carry_t = stacked(carry).astype(bf16)
    last = stacked(within)[127:128, :]
    copies[5].wait()
    b_t = b_buf[...].astype(f32).T.astype(bf16)
    copies[6].wait()
    grown = jnp.exp(within)
    rows = [weight_buf[level] * grown for level in range(1, LEVELS + 1)]
    gains = jnp.concatenate(rows + [jnp.zeros((16, 128), f32)], axis=0).T.astype(bf16)
    carry_ref[...] = carry_t
    last_ref[...] = jnp.broadcast_to(last, (8, 128))
    bt_ref[...] = b_t
    gains_ref[...] = gains
    copies[7].wait()
    for c in copies[:3]:
        c.wait()
    messages = zip((far_ref, cross_ref, beside_ref), (far_side, cross_side, beside_side))
    for i, (mask, refs) in enumerate(zip(FIRST, messages)):
        part = spots()[2] ^ mask
        worker_message(part, x_buf[i], carry_t, last, b_t, gains, c_buf[...], *refs)


def second_kernel(
    x_ref, c_ref, carry_ref, last_ref, bt_ref, gains_ref, own_ref, own_side,
    x_buf, c_buf, sems,
):
    copies = column_copies(SECOND, x_ref, x_buf, sems)
    copies.append(pltpu.make_async_copy(c_ref, c_buf, sems.at[1]))
    for c in copies:
        c.start()
    for c in copies:
        c.wait()
    worker_message(
        spots()[2], x_buf[0], carry_ref[...], last_ref[0:1, :], bt_ref[...], gains_ref[...], c_buf[...], own_ref, own_side
    )


def local_kernel(
    x_hbm, b_hbm, c_hbm, step_hbm, weight_hbm, gate_hbm, within_ref, out_ref, silu_ref,
    x_ref, b_ref, c_ref, step_ref, weight_ref, gate_ref, sems,
):
    pairs = (
        (x_hbm, x_ref), (b_hbm, b_ref), (c_hbm, c_ref), (step_hbm, step_ref),
        (weight_hbm.at[0], weight_ref), (gate_hbm, gate_ref),
    )
    copies = [pltpu.make_async_copy(*p, sems.at[i]) for i, p in enumerate(pairs)]
    for c in copies:
        c.start()
    for c in copies:
        c.wait()
    scores = lax.dot_general(
        c_ref[...], b_ref[...], (((1,), (1,)), ((), ())), preferred_element_type=f32
    )
    scores = jnp.where(iota((128, 128), 0) >= iota((128, 128), 1), scores, 0.0)
    pad = jnp.zeros((128 - HEADS, 128), f32)
    within = within_ref[...]
    within_t = jnp.concatenate([within, pad], axis=0).T
    weight_t = jnp.concatenate([weight_ref[...], pad], axis=0).T
    step = step_ref[...]
    left = iota((128, 128), 1) < HEADDIM
    zero = jnp.zeros((128, 128), bf16)

    def mixing(h):
        gap = jnp.minimum(within_t[:, h : h + 1] - within[h : h + 1, :], 0.0)
        gain = weight_t[:, h : h + 1] * jnp.exp(gap)
        return (gain * scores * step[h : h + 1, :]).astype(bf16)

    for pair in range(HEADS // 2):
        cols = slice(pair * 128, (pair + 1) * 128)
        x = x_ref[:, cols]
        both = jnp.concatenate([mixing(2 * pair), mixing(2 * pair + 1)], axis=1)
        sides = jnp.concatenate([jnp.where(left, x, zero), jnp.where(left, zero, x)], axis=0)
        out_ref[:, cols] = dot(both, sides)
        gate = gate_ref[:, cols].astype(f32)
        silu_ref[:, cols] = gate / (1.0 + jnp.exp(-gate))


def total_of(meta, tile):
    return meta[3 * tile : 3 * tile + 1] + meta[3 * tile + 1 : 3 * tile + 2] + meta[3 * tile + 2 : 3 * tile + 3]


def put_total(meta, tile, total):
    row = iota((META, 128), 0)
    for k, p in enumerate(three(total)):
        meta = jnp.where(row == 3 * tile + k, p.astype(f32), meta)
    return meta


def tile_rows(tile):
    return slice(tile * STATE, (tile + 1) * STATE)


def group_kernel(*refs):
    got, (first_ref, second_ref, parts_ref) = refs[:PLACES], refs[PLACES:]
    for mask, ref in zip(MASKS, got):
        parts_ref[spots()[2] ^ mask] = ref[...]
    metas = [parts_ref[j, BODY:, :].astype(f32) for j in range(PLACES)]
    for tiles, out_ref in ((range(AHEAD), first_ref), (range(AHEAD, TILES), second_ref)):
        meta = jnp.zeros((META, 128), f32)
        for tile in tiles:
            rows = tile_rows(tile)
            t = [total_of(m, tile) for m in metas]
            acc = parts_ref[0, rows, :].astype(f32)
            for j in range(1, PLACES):
                acc = jnp.exp(t[j]) * acc + parts_ref[j, rows, :].astype(f32)
            out_ref[tile_rows(tile - tiles[0]), :] = acc.astype(bf16)
            meta = put_total(meta, tile - tiles[0], t[0] + t[1] + t[2] + t[3])
        out_ref[len(tiles) * STATE :, :] = meta.astype(bf16)


def flag(cond):
    return jnp.where(cond, 1.0, 0.0).astype(f32)


def joined(later, own, own_t, other, other_t):
    return jnp.exp(other_t * (1.0 - later)) * own + jnp.exp(own_t * later) * other


def pair_kernel(own_ref, other_ref, out_ref):
    later = flag(spots()[0] % 2 == 1)
    end = AHEAD * STATE
    own_meta, other_meta = own_ref[end:, :].astype(f32), other_ref[end:, :].astype(f32)
    meta = jnp.zeros((META, 128), f32)
    for tile in range(AHEAD):
        rows = tile_rows(tile)
        own_t, other_t = total_of(own_meta, tile), total_of(other_meta, tile)
        own, other = own_ref[rows, :].astype(f32), other_ref[rows, :].astype(f32)
        out_ref[rows, :] = joined(later, own, own_t, other, other_t).astype(bf16)
        meta = put_total(meta, tile, own_t + other_t)
    out_ref[end:, :] = meta.astype(bf16)


def both_kernel(own_ref, opposite_ref, out_ref):
    out_ref[0] = own_ref[...]
    out_ref[1] = opposite_ref[...]


def row_kernel(
    next_ref, pair_ref, far_ref, own_ref, opposite_ref, beside_ref, next_out, far_out, total_out
):
    odd, upper = flag(spots()[0] % 2 == 1), flag(spots()[0] >= 2)
    next_sum = jnp.zeros((META, 128), f32)
    far_sum, total_sum = next_sum, next_sum
    end, late = AHEAD * STATE, (TILES - AHEAD) * STATE
    next_meta, pair_meta, far_meta = (r[end:, :].astype(f32) for r in (next_ref, pair_ref, far_ref))
    own_meta, opposite_meta = own_ref[late:, :].astype(f32), opposite_ref[late:, :].astype(f32)
    beside_meta, last_meta = beside_ref[0, late:, :].astype(f32), beside_ref[1, late:, :].astype(f32)
    for tile in range(TILES):
        rows = tile_rows(tile)
        if tile < AHEAD:
            next_t, pair_t, far_t = (total_of(m, tile) for m in (next_meta, pair_meta, far_meta))
            next_out[rows, :] = next_ref[rows, :]
            far_out[rows, :] = far_ref[rows, :]
            pair, far = pair_ref[rows, :].astype(f32), far_ref[rows, :].astype(f32)
        else:
            spot = tile_rows(tile - AHEAD)
            own_t, next_t, opposite_t, last_t = (
                total_of(m, tile - AHEAD) for m in (own_meta, beside_meta, opposite_meta, last_meta)
            )
            own, opposite = own_ref[spot, :].astype(f32), opposite_ref[spot, :].astype(f32)
            beside, last = beside_ref[0, spot, :].astype(f32), beside_ref[1, spot, :].astype(f32)
            pair = joined(odd, own, own_t, beside, next_t)
            far = joined(1.0 - odd, opposite, opposite_t, last, last_t)
            pair_t, far_t = own_t + next_t, opposite_t + last_t
            next_out[rows, :] = beside_ref[0, spot, :]
            far_out[rows, :] = far.astype(bf16)
        total_out[rows, :] = joined(upper, pair, pair_t, far, far_t).astype(bf16)
        next_sum = put_total(next_sum, tile, next_t)
        far_sum = put_total(far_sum, tile, far_t)
        total_sum = put_total(total_sum, tile, pair_t + far_t)
    for out, meta in ((next_out, next_sum), (far_out, far_sum), (total_out, total_sum)):
        out[BODY:, :] = meta.astype(bf16)


def split(v):
    hi = v.astype(bf16)
    return jnp.concatenate([hi, (v - hi.astype(f32)).astype(bf16)], axis=0)


def wide(pieces):
    return pieces[0] if len(pieces) == 1 else jnp.concatenate(pieces, axis=1)


def gain_spread(tiles, level):
    slot = iota((128, 128), 0)
    side = jnp.where(iota((128, 128), 1) >= HEADDIM, 1, 0)
    return [
        wide([ones_where(slot == base + level * PART_HEADS + 2 * tile + side) for tile in tiles])
        for base in (0, 64)
    ]


def spread_gain(gains, spread):
    return jnp.concatenate([dot(gains, s) for s in spread], axis=0)


def block_lead(metas, place, tiles):
    return wide(
        [
            jnp.exp(sum(flag(place > j) * total_of(metas[j], tile) for j in range(PLACES - 1)))
            for tile in tiles
        ]
    )


def near_kernel(
    parts_ref, next_ref, pair_ref, far_side, cross_side, beside_side, own_side,
    out_ref, c_ref, gain_ref, gains_ref,
):
    group = spots()[0]
    for mask, ref in zip(MASKS, (far_side, cross_side, beside_side, own_side)):
        c_ref[spots()[2] ^ mask] = ref[:128, :]
        gains_ref[spots()[2] ^ mask] = ref[128:, :]
    part_metas = [parts_ref[j, BODY:, :].astype(f32) for j in range(PLACES)]
    next_meta = next_ref[BODY:, :].astype(f32)
    odd, upper, third = flag(group % 2 == 1), flag(group >= 2), flag(group == 3)
    for start in range(0, TILES, 2):
        tiles = range(start, min(start + 2, TILES))
        low_b, mid_b, high_b, b3, b4, skip = [], [], [], [], [], []
        for tile in tiles:
            rows = tile_rows(tile)
            t = [total_of(m, tile) for m in part_metas]
            s0, s1 = parts_ref[0, rows, :], parts_ref[1, rows, :]
            low_b.append(s0)
            mid_b.append(split(jnp.exp(t[1]) * s0.astype(f32) + s1.astype(f32)))
            high_b.append(parts_ref[2, rows, :])
            skip.append(jnp.exp(t[2]))
            b3.append(split(odd * next_ref[rows, :].astype(f32)))
            w4 = upper * jnp.exp(third * total_of(next_meta, tile))
            b4.append(split(w4 * pair_ref[rows, :].astype(f32)))
        spread = [gain_spread(tiles, level) for level in range(LEVELS)]
        low_w, mid_w, high_w = wide(low_b), wide(mid_b), wide(high_b)
        b3_w, b4_w = wide(b3), wide(b4)
        lanes = slice(start * 128, (start + len(tiles)) * 128)
        for place in range(PLACES):
            c = c_ref[place]
            cc = jnp.concatenate([c, c], axis=1)
            gains = gains_ref[place]
            acc = spread_gain(gains, spread[2]) * dot(cc, b3_w)
            acc = acc + spread_gain(gains, spread[3]) * dot(cc, b4_w)
            lead = block_lead(part_metas, place, tiles)
            for k in range(2):
                gain_ref[place, k, :, lanes] = spread_gain(gains, spread[4 + k]) * lead
            acc = acc * lead
            if place == 1:
                acc = acc + spread_gain(gains, spread[0]) * dot(c, low_w)
            if place == 3:
                acc = acc + spread_gain(gains, spread[0]) * dot(c, high_w)
            if place >= 2:
                term = spread_gain(gains, spread[1]) * dot(cc, mid_w)
                acc = acc + (term * wide(skip) if place == 3 else term)
            out_ref[place, :, lanes] = acc


def far_kernel(
    masks, c_ref, gain_ref, next_ref, pair_ref, r1_ref, r2_ref, r3_ref, near_ref, *out_refs
):
    group, row = spots()[:2]
    metas = [r[BODY:, :].astype(f32) for r in (next_ref, pair_ref)]
    odd_group, upper_group = flag(group % 2 == 1), flag(group >= 2)
    row_metas = [r[BODY:, :].astype(f32) for r in (r1_ref, r2_ref)]
    odd, upper = flag(row % 2 == 1), flag(row >= 2)
    second, third = flag(row == 2), flag(row == 3)
    for start in range(0, TILES, 2):
        tiles = range(start, min(start + 2, TILES))
        b5, b6 = [], []
        for tile in tiles:
            rows = tile_rows(tile)
            t = [total_of(m, tile) for m in metas]
            t1, t2 = (total_of(m, tile) for m in row_metas)
            lead = jnp.exp(odd_group * t[0] + upper_group * t[1])
            v1, v2, v3 = (r[rows, :].astype(f32) for r in (r1_ref, r2_ref, r3_ref))
            b5.append(split((lead * odd) * v1))
            w2, w3 = lead * upper * jnp.exp(t1), lead * third * jnp.exp(t1 + t2)
            b6.append(split((lead * second) * v1 + w2 * v2 + w3 * v3))
        b5_w, b6_w = wide(b5), wide(b6)
        lanes = slice(start * 128, (start + len(tiles)) * 128)
        for mask, out_ref in zip(masks, out_refs):
            place = spots()[2] ^ mask
            c = c_ref[place]
            cc = jnp.concatenate([c, c], axis=1)
            acc = gain_ref[place, 0, :, lanes] * dot(cc, b5_w)
            acc = acc + gain_ref[place, 1, :, lanes] * dot(cc, b6_w)
            acc = acc + near_ref[place, :, lanes]
            out_ref[:, lanes] = acc.astype(bf16)


def gate_kernel(local_ref, silu_ref, *refs):
    reached, (gated_ref, square_ref) = refs[:PLACES], refs[PLACES:]
    acc = jnp.zeros((128, 128), f32)
    for mask, reached_ref in zip(MASKS, reached):
        start = (spots()[2] ^ mask) * PART
        for tile in range(TILES):
            cols = pl.ds(pl.multiple_of(start + tile * 128, 128), 128)
            mixed = local_ref[:, cols] + reached_ref[:, tile * 128 : (tile + 1) * 128].astype(f32)
            gated = (mixed * silu_ref[:, cols]).astype(bf16)
            gated_ref[:, cols] = gated
            full = gated.astype(f32)
            acc = acc + full * full
    square_ref[...] = acc


def norm_kernel(gated_ref, own_ref, other_ref, weight_ref, out_ref):
    mean = jnp.sum(own_ref[...] + other_ref[...], axis=1, keepdims=True) / (2.0 * COLS)
    inverse = jnp.broadcast_to(lax.rsqrt(mean + 1e-05), (128, 128))
    for pair in range(HEADS // 2):
        cols = slice(pair * 128, (pair + 1) * 128)
        out_ref[:, cols] = (
            gated_ref[:, cols].astype(f32) * inverse * weight_ref[:, cols]
        ).astype(bf16)


def call(kernel, name, outs, *args, far=0, scratch=(), flops=10**8, size=4 * 10**6, vmem=VMEM):
    whole = pl.BlockSpec(memory_space=pltpu.VMEM)
    specs = [pl.BlockSpec(memory_space=pltpu.HBM)] * far + [whole] * (len(args) - far)
    return pl.pallas_call(
        kernel,
        name=name,
        in_specs=specs,
        out_specs=[whole] * len(outs),
        out_shape=[jax.ShapeDtypeStruct(*o) for o in outs],
        scratch_shapes=list(scratch),
        cost_estimate=pl.CostEstimate(flops=flops, bytes_accessed=size, transcendentals=0),
        compiler_params=pltpu.CompilerParams(vmem_limit_bytes=vmem),
    )(*args)


def spot_of(index):
    return index // 16, index // 4 % 4, index % 4


def index_of(row, group, place):
    return row * 16 + group * 4 + place


def to_group(value, partner):
    pairs = []
    for index in range(ROWS * GROUPS * PLACES):
        row, group, place = spot_of(index)
        pairs.append((index, index_of(row, partner(group), place)))
    return lax.ppermute(value, "ctx", pairs)


def to_row(value, shift):
    pairs = []
    for index in range(ROWS * GROUPS * PLACES):
        row, group, place = spot_of(index)
        if row + shift < ROWS:
            pairs.append((index, index_of(row + shift, group, place)))
    return lax.ppermute(value, "ctx", pairs)


def to_place(value, mask):
    if not mask:
        return value
    return lax.ppermute(value, "ctx", [(i, i ^ mask) for i in range(ROWS * GROUPS * PLACES)])


def on_device(
    mixer_input,
    gate_input,
    input_proj,
    output_proj,
    step_size,
    decay_log,
    level_weight,
    norm_weight,
):
    message, extra = ((MSG, 128), bf16), ((EXTRA, 128), bf16)
    far, cross, beside, far_side, cross_side, beside_side, within, carry_t, last, b_t, gains = call(
        first_kernel,
        "first_states",
        [
            message,
            message,
            message,
            extra,
            extra,
            extra,
            ((HEADS, 128), f32),
            ((128, 128), bf16),
            ((8, 128), f32),
            ((128, 128), bf16),
            ((128, 256), bf16),
        ],
        mixer_input,
        input_proj,
        output_proj,
        decay_log,
        step_size,
        level_weight,
        far=6,
        vmem=60 * 2**20,
        scratch=[
            pltpu.VMEM((len(FIRST), 128, PART), bf16),
            pltpu.VMEM((128, 128), bf16),
            pltpu.VMEM((128, 128), bf16),
            pltpu.VMEM((HEADS, 128), f32),
            pltpu.VMEM((HEADS, 128), f32),
            pltpu.VMEM((LEVELS + 1, HEADS, 128), f32),
            pltpu.SemaphoreType.DMA((8,)),
        ],
    )
    own, own_side = call(
        second_kernel,
        "second_states",
        [message, extra],
        mixer_input,
        output_proj,
        carry_t,
        last,
        b_t,
        gains,
        far=2,
        flops=4 * 10**10,
        scratch=[
            pltpu.VMEM((len(SECOND), 128, PART), bf16),
            pltpu.VMEM((128, 128), bf16),
            pltpu.SemaphoreType.DMA((2,)),
        ],
    )
    local, silu = call(
        local_kernel,
        "local_part",
        [((128, COLS), f32), ((128, COLS), f32)],
        mixer_input,
        input_proj,
        output_proj,
        step_size,
        level_weight,
        gate_input,
        within,
        far=6,
        scratch=[
            pltpu.VMEM((128, COLS), bf16),
            pltpu.VMEM((128, 128), bf16),
            pltpu.VMEM((128, 128), bf16),
            pltpu.VMEM((HEADS, 128), f32),
            pltpu.VMEM((HEADS, 128), f32),
            pltpu.VMEM((128, COLS), bf16),
            pltpu.SemaphoreType.DMA((6,)),
        ],
        flops=10**10,
        size=10**7,
    )
    got = [to_place(v, mask) for mask, v in zip(MASKS, (far, cross, beside, own))]
    ahead = ((AHEAD * STATE + META, 128), bf16)
    behind = (((TILES - AHEAD) * STATE + META, 128), bf16)
    whole = ((BODY + META, 128), bf16)
    sums, late_sums, parts = call(
        group_kernel,
        "group_state",
        [ahead, behind, ((PLACES, MSG, 128), bf16)],
        *got,
    )
    opposite = to_group(late_sums, lambda g: 3 - g)
    (both,) = call(
        both_kernel, "two_states", [((2,) + behind[0], bf16)], late_sums, opposite
    )
    beside = to_group(sums, lambda g: g ^ 1)
    (pair,) = call(pair_kernel, "pair_state", [ahead], sums, beside)
    late_beside = to_group(both, lambda g: g ^ 1)
    other_pair = to_group(pair, lambda g: 3 - g)
    sides, _ = lax.optimization_barrier(((far_side, cross_side, beside_side), sums))
    sides = [to_place(v, mask) for mask, v in zip(MASKS, sides)] + [own_side]
    neighbour, other_pair, total = call(
        row_kernel,
        "row_state",
        [whole, whole, whole],
        beside,
        pair,
        other_pair,
        late_sums,
        opposite,
        late_beside,
    )
    rows = [to_row(total, k) for k in (1, 2, 3)]
    near, c_all, far_gains = call(
        near_kernel,
        "near_levels",
        [((PLACES, 128, PART), f32), ((PLACES, 128, 128), bf16), ((PLACES, 2, 128, PART), f32)],
        parts,
        neighbour,
        other_pair,
        *sides,
        scratch=[pltpu.VMEM((PLACES, 64, 128), bf16)],
        flops=10**10,
    )
    reached = []
    for masks in (FIRST, SECOND):
        reached += call(
            functools.partial(far_kernel, masks),
            "far_levels",
            [((128, PART), bf16)] * len(masks),
                c_all,
            far_gains,
            neighbour,
            other_pair,
            *rows,
            near,
                flops=10**10,
        )
    back = [to_place(v, mask) for mask, v in zip(MASKS, reached)]
    gated, square = call(
        gate_kernel,
        "gate",
        [((128, COLS), bf16), ((128, 128), f32)],
        local,
        silu,
        *back,
    )
    other = lax.ppermute(square, "head", [(0, 1), (1, 0)])
    (out,) = call(
        norm_kernel,
        "norm",
        [((128, COLS), bf16)],
        gated,
        square,
        other,
        norm_weight.reshape(1, COLS),
    )
    return out


def solution(mesh):
    in_specs = (
        P(("seq", "ctx"), "head"),
        P(("seq", "ctx"), "head"),
        P(("seq", "ctx"), None),
        P(("seq", "ctx"), None),
        P("head", ("seq", "ctx")),
        P("head", ("seq", "ctx")),
        P(None, "head", ("seq", "ctx")),
        P("head"),
    )
    out_specs = P(("seq", "ctx"), "head")
    return jax.shard_map(
        on_device, mesh=mesh, in_specs=in_specs, out_specs=out_specs, check_vma=False
    )
```
